256 devices in a mesh: panel: 4 (over y), front: 64 (over x, z, core).
Axes of the slice: x: 4, y: 4, z: 8, core: 2. Of those that a mesh axis runs over, the one named last changes fastest.
Arguments:
- leaf_rhs: float32 [4, 64, 2, 32, 1280], P('panel', 'front'), may hold values from -6 to 6
- sep_rhs: float32 [4, 2, 32, 1024], P('panel', None, None, 'front'), may hold values from -6 to 6
- leaf_inverse: bfloat16 [4, 64, 2, 1280, 1280], P('panel', 'front'), may hold values from -0.15625 to 0.15625
- coupling: bfloat16 [4, 64, 2, 1280, 128], P('panel', 'front'), may hold values from -0.15625 to 0.15625
- sep_index: int32 [4, 64, 128], P('panel', 'front'), may hold values from 0 to 1023, as said below
- sep_inverse: bfloat16 [4, 2, 1024, 1024], P('panel', None, None, 'front'), may hold values from -0.1875 to 0.1875
Outputs:
- leaf_solution: float32 [4, 64, 2, 32, 1280], P('panel', 'front')
- sep_solution: float32 [4, 2, 32, 1024], P('panel', None, None, 'front')
The draws below stay inside these ranges and needn't reach their ends.
Inputs may be any that keep to these rules, and one draw needn't show every extreme that they name: `sep_index`: within one leaf no separator unknown repeats, and every separator unknown of a panel is coupled to exactly 8 leaves.
All inputs are finite; a program needn't handle non-finite values.
Results may differ from the reference program's by a relative error of at most 0.035.
Values may be sent and summed in bfloat16 or wider, within the bound.
A program may use at most 64 MiB of HBM per device.

```python
import jax
import jax.numpy as jnp
from jax import lax

M = 1280
BW = 128
LAYER = 128
SEP_DEV = 16
RHS = 32
PANELS = 4
LEAVES = 64
SEP = 1024


def draw_sep_index(key, part):
    key = jax.random.fold_in(key, 7)
    rounds = BW // SEP_DEV
    keys = jax.random.split(key, PANELS * rounds)
    orders = jax.vmap(lambda single: jax.random.permutation(single, SEP))(keys)
    return orders.reshape(PANELS, LEAVES, BW).astype(jnp.int32)


def shard_levels(rng, extent, cuts, smallest, largest):
    def one(position, blocks):
        draws = jax.random.uniform(jax.random.fold_in(jax.random.fold_in(rng, 6), position), (blocks,), jnp.float32, smallest / len(cuts), largest / len(cuts))
        return jnp.repeat(jnp.exp(draws), extent[position] // blocks).reshape((-1,) + (1,) * (len(extent) - position - 1))

    loudness = one(*cuts[0])
    for cut in cuts[1:]:
        loudness = loudness * one(*cut)
    return loudness


def scatter_about(own_key, shape, spread, limit, shards=(), dtype=jnp.bfloat16):
    drawn = jax.random.normal(own_key, shape, jnp.float32) * spread
    if len(shards) > 0:
        drawn = shard_levels(own_key, shape, shards, -0.22, 0.18) * drawn
    return jnp.clip(drawn, min=-limit, max=limit).astype(dtype)


def setup_inputs(seed: int = 0) -> dict:
    seeds = jax.random.split(jax.random.key(seed), 7)
    leaf_rhs = scatter_about(seeds[0], (PANELS, LEAVES, 2, RHS, M), 1.0, 6.0, ((0, 4), (1, 64)), jnp.float32)
    sep_rhs = scatter_about(seeds[1], (PANELS, 2, RHS, SEP), 1.0, 6.0, ((0, 4), (3, 64)), jnp.float32)
    leaf_inverse = scatter_about(seeds[2], (PANELS, LEAVES, 2, M, M), M ** -0.5, 0.15625, ((0, 4), (1, 64)))
    coupling = scatter_about(seeds[3], (PANELS, LEAVES, 2, M, BW), M ** -0.5, 0.15625, ((0, 4), (1, 64)))
    sep_index = draw_sep_index(jax.random.fold_in(seeds[6], 71), 0)
    sep_inverse = scatter_about(seeds[5], (PANELS, 2, SEP, SEP), SEP ** -0.5, 0.1875, ((0, 4), (3, 64)))
    return dict(leaf_rhs=leaf_rhs, sep_rhs=sep_rhs, leaf_inverse=leaf_inverse, coupling=coupling, sep_index=sep_index, sep_inverse=sep_inverse)


def complex_rows(vector, matrix):
    count = vector.shape[1]
    flat = vector.reshape(2 * count, vector.shape[2])
    real_part = jnp.dot(flat, matrix[0], preferred_element_type=jnp.float32)
    imag_part = jnp.dot(flat, matrix[1], preferred_element_type=jnp.float32)
    return jnp.stack([real_part[:count] - imag_part[count:], imag_part[:count] + real_part[count:]])


def complex_rows_back(vector, matrix):
    count = vector.shape[1]
    flat = vector.reshape(2 * count, vector.shape[2])
    dims = (((1,), (1,)), ((), ()))
    real_part = lax.dot_general(flat, matrix[0], dims, preferred_element_type=jnp.float32)
    imag_part = lax.dot_general(flat, matrix[1], dims, preferred_element_type=jnp.float32)
    return jnp.stack([real_part[:count] - imag_part[count:], imag_part[:count] + real_part[count:]])


def leaf_apply(pair):
    return complex_rows(pair[1].astype(jnp.bfloat16), pair[0])


def back_apply(pair):
    return complex_rows_back(pair[1].astype(jnp.bfloat16), pair[0])


def solve_panel(inverse, coupling, index, sep_inverse, leaf_side, sep_side):
    first = lax.map(leaf_apply, (inverse, leaf_side))
    toward = lax.map(leaf_apply, (coupling, first))
    leaves = toward.shape[0]
    flat = jnp.transpose(toward, (1, 2, 0, 3)).reshape(2, toward.shape[2], leaves * toward.shape[3])
    summed = jnp.zeros(sep_side.shape, jnp.float32).at[:, :, index.reshape(-1)].add(flat)
    reduced = sep_side - summed
    sep_sol = complex_rows(reduced.astype(jnp.bfloat16), sep_inverse)
    picked = jnp.transpose(sep_sol[:, :, index], (2, 0, 1, 3))
    back = lax.map(back_apply, (coupling, picked))
    corr = lax.map(leaf_apply, (inverse, back))
    return first - corr, sep_sol


def reference(leaf_rhs, sep_rhs, leaf_inverse, coupling, sep_index, sep_inverse):
    cells = leaf_rhs.shape[4]
    forward_leaf = []
    forward_sep = []
    given = leaf_rhs[0]
    for panel in range(PANELS):
        leaf_sol, sep_sol = solve_panel(leaf_inverse[panel], coupling[panel], sep_index[panel], sep_inverse[panel], given, sep_rhs[panel])
        forward_leaf.append(leaf_sol)
        forward_sep.append(sep_sol)
        if panel + 1 < PANELS:
            given = leaf_rhs[panel + 1].at[:, :, :, :LAYER].add(leaf_sol[:, :, :, cells - LAYER:])
    final_leaf = [None] * PANELS
    final_sep = [None] * PANELS
    final_leaf[PANELS - 1] = forward_leaf[PANELS - 1]
    final_sep[PANELS - 1] = forward_sep[PANELS - 1]
    for panel in range(PANELS - 2, -1, -1):
        lifted = jnp.zeros(leaf_rhs[panel].shape, jnp.float32).at[:, :, :, cells - LAYER:].set(final_leaf[panel + 1][:, :, :, :LAYER])
        zero_sep = jnp.zeros(sep_rhs[panel].shape, jnp.float32)
        leaf_sol, sep_sol = solve_panel(leaf_inverse[panel], coupling[panel], sep_index[panel], sep_inverse[panel], lifted, zero_sep)
        final_leaf[panel] = forward_leaf[panel] + leaf_sol
        final_sep[panel] = forward_sep[panel] + sep_sol
    return jnp.stack(final_leaf), jnp.stack(final_sep)
```

```python
import jax
import jax.numpy as jnp
from jax import lax
from jax.experimental import pallas as pl
from jax.experimental.pallas import tpu as pltpu
from jax.sharding import PartitionSpec as P

MESH = pl.DeviceIdType.MESH
F32 = jnp.float32
BF16 = jnp.bfloat16
FACE = 128
CELLS = 1280
SEP = 1024
BLOCK = 256
NT = (((1,), (1,)), ((), ()))
TN = (((0,), (0,)), ((), ()))

T_F, O_F, D_F, O_B, D_FF, T_B, D_B = range(7)
X_SINV, X_IDX, X_BASE, X_MAT, X_PART, X_SOL, X_YF, X_YB, X_FINAL, X_COUNT = 0, 1, 2, 3, 10, 13, 16, 17, 18, 19


def dot(a, b):
    return jnp.dot(a, b, preferred_element_type=F32)


def kernel(rhs_ref, bs_ref, inv_hbm, cc_ref, idx_ref, sinv_hbm, out_ref, sep_ref,
           inv, w, gm, gs, gi, pt, stage, kb, pbuf, sbuf, yout, yin, fstage, fk, accl, accf, stot, lsem, ssem, rsem):
    p = lax.axis_index("panel")
    front = lax.axis_index("front")
    x, z, c = front // 16, lax.rem(front // 2, 8), lax.rem(front, 2)
    g = x * 2 + c
    first_panel, last_panel = p == 0, p == 3

    def z_peer(k):
        other = lax.rem(z + k, 8)
        return other, (p, (x * 8 + other) * 2 + c)

    def g_peer(k):
        other = lax.rem(g + k, 8)
        return other, (p, ((other // 2) * 8 + z) * 2 + lax.rem(other, 2))

    for block in range(5):
        rows = pl.ds(block * BLOCK, BLOCK)
        pltpu.make_async_copy(inv_hbm.at[:, rows], inv.at[:, rows], lsem.at[block]).start()
    own_sinv = pltpu.make_async_copy(sinv_hbm, gs.at[:, z], lsem.at[5])
    own_sinv.start()

    barrier = pltpu.get_barrier_semaphore()
    for k in range(1, 8):
        pl.semaphore_signal(barrier, inc=1, device_id=z_peer(k)[1], device_id_type=MESH)
        pl.semaphore_signal(barrier, inc=1, device_id=g_peer(k)[1], device_id_type=MESH)

    @pl.when(p > 0)
    def _():
        pl.semaphore_signal(barrier, inc=1, device_id=(p - 1, front), device_id_type=MESH)

    @pl.when(p < 3)
    def _():
        pl.semaphore_signal(barrier, inc=1, device_id=(p + 1, front), device_id_type=MESH)

    pl.semaphore_wait(barrier, 14 + (p > 0).astype(jnp.int32) + (p < 3).astype(jnp.int32))

    def send(src, dst, which, device):
        pltpu.make_async_remote_copy(
            src_ref=src, dst_ref=dst, send_sem=ssem.at[which], recv_sem=rsem.at[which], device_id=device, device_id_type=MESH
        ).start()

    def send_z(src, dst, which):
        for k in range(1, 8):
            send(src, dst, which, z_peer(k)[1])

    def send_g(src, dst, which):
        for k in range(1, 8):
            send(src, dst, which, g_peer(k)[1])

    def wait(ref, sem):
        pltpu.make_async_copy(ref, ref, sem).wait()

    send_z(sinv_hbm, gs.at[:, z], X_SINV)
    gi[z] = idx_ref[...]
    send_z(idx_ref, gi.at[z], X_IDX)

    flat = rhs_ref[...].reshape(64, CELLS).astype(BF16)
    towards = jnp.zeros((64, 2 * FACE), F32)
    faces = [jnp.zeros((64, 2 * FACE), F32) for _ in range(2)]
    outs = [jnp.zeros((2 * FACE, 2 * FACE), F32) for _ in range(2)]
    link = jnp.concatenate([cc_ref[0], cc_ref[1]], axis=1)
    for block in range(5):
        rows = pl.ds(block * BLOCK, BLOCK)
        pltpu.make_async_copy(inv_hbm.at[:, rows], inv.at[:, rows], lsem.at[block]).wait()
        real = dot(inv[0, rows], link)
        imag = dot(inv[1, rows], link)
        part = jnp.concatenate(
            [real[:, :FACE] - imag[:, FACE:], real[:, FACE:] + imag[:, :FACE]], axis=1
        ).astype(BF16)
        w[rows] = part
        some = flat[:, block * BLOCK : (block + 1) * BLOCK]
        towards = towards + dot(some, part)
        link_rows = link[block * BLOCK : (block + 1) * BLOCK]
        for side, start in enumerate((0, CELLS - FACE)):
            cols = pl.ds(start, FACE)
            both = jnp.concatenate([inv[0, rows, cols], inv[1, rows, cols]], axis=1)
            faces[side] = faces[side] + dot(some, both)
            outs[side] = outs[side] + lax.dot_general(link_rows, both, TN, preferred_element_type=F32)

    def combine(value):
        return jnp.concatenate(
            [value[:32, :FACE] - value[32:, FACE:], value[32:, :FACE] + value[:32, FACE:]], axis=0
        )

    pieces = [combine(towards), bs_ref[...].reshape(64, FACE), combine(faces[0]), combine(faces[1])]
    for other in range(8):
        for item, value in enumerate(pieces):
            stage[other, item] = jnp.concatenate(
                [value[4 * other : 4 * other + 4], value[32 + 4 * other : 36 + 4 * other]], axis=0
            )
    for k in range(1, 8):
        other, device = z_peer(k)
        send(stage.at[other], kb.at[z], X_BASE, device)
    kb[z] = stage[z]

    for side, slot in ((0, O_B), (1, O_F)):
        value = outs[side]
        gm[slot, z] = jnp.concatenate(
            [value[:FACE, :FACE] - value[FACE:, FACE:], value[:FACE, FACE:] + value[FACE:, :FACE]], axis=1
        ).astype(BF16)
    low, high = pl.ds(0, FACE), pl.ds(CELLS - FACE, FACE)
    gm[T_F, z] = w[low]
    gm[T_B, z] = w[high]
    for slot, r, q in ((D_F, low, high), (D_FF, low, low), (D_B, high, low)):
        gm[slot, z] = jnp.concatenate([inv[0, r, q], inv[1, r, q]], axis=1)

    needed = {
        T_F: p > 0, O_F: p < 3, D_F: (p > 0) & (p < 3), O_B: p > 0, D_FF: p > 0, T_B: p < 3, D_B: (p > 0) & (p < 3)
    }
    for slot in range(7):
        @pl.when(needed[slot])
        def _(slot=slot):
            send_z(gm.at[slot, z], gm.at[slot, z], X_MAT + slot)

    def arrived(slot):
        wait(gm.at[slot, pl.ds(0, 7)], rsem.at[X_MAT + slot])

    wait(gi.at[pl.ds(0, 7)], rsem.at[X_IDX])
    unknown = lax.broadcasted_iota(jnp.int32, (SEP, FACE), 0)
    for leaf in range(8):
        row = gi[leaf][0:1, :]
        pt[:, leaf * FACE : (leaf + 1) * FACE] = jnp.where(unknown == row, 1.0, 0.0).astype(BF16)

    sign = jnp.where(lax.broadcasted_iota(jnp.int32, (8, SEP), 0) < 4, -1.0, 1.0)

    def leafwise(vector, slot):
        parts = [dot(vector[:, leaf * FACE : (leaf + 1) * FACE], gm[slot, leaf]) for leaf in range(8)]
        direct = jnp.concatenate([v[:, :FACE] for v in parts], axis=1)
        crossed = jnp.concatenate([v[:, FACE:] for v in parts], axis=1)
        return direct + sign * jnp.roll(crossed, 4, axis=0)

    def fold(value):
        half = value.shape[1] // 2
        return jnp.concatenate([value[:, :half], value[:, half:]], axis=0).astype(BF16)

    def unfold(value):
        value = value.astype(F32)
        return jnp.concatenate([value[:8], value[8:]], axis=1)

    def scatter(value):
        return lax.dot_general(value.astype(BF16), pt[...], NT, preferred_element_type=F32)

    def share(partial, turn):
        pbuf[turn, g] = fold(partial)
        send_g(pbuf.at[turn, g], pbuf.at[turn, g], X_PART + turn)

    def solve(turn):
        wait(pbuf.at[turn, pl.ds(0, 7)], rsem.at[X_PART + turn])
        total = pbuf[turn, 0].astype(F32)
        for other in range(1, 8):
            total = total + pbuf[turn, other].astype(F32)
        reduced = unfold(total).astype(BF16)
        both = lax.dot_general(reduced, gs[...].reshape(2 * FACE, SEP), NT, preferred_element_type=F32)
        mine = both[:, :FACE] + sign[:, :FACE] * jnp.roll(both[:, FACE:], 4, axis=0)
        sbuf[turn, g] = mine
        send_g(sbuf.at[turn, g], sbuf.at[turn, g], X_SOL + turn)
        wait(sbuf.at[turn, pl.ds(0, 7)], rsem.at[X_SOL + turn])
        return jnp.concatenate([sbuf[turn, other] for other in range(8)], axis=1)

    def gather(value):
        return dot(value.astype(BF16), pt[...])

    wait(kb.at[pl.ds(0, 7)], rsem.at[X_BASE])
    own = -scatter(jnp.concatenate([kb[leaf, 0] for leaf in range(8)], axis=1))
    given = kb[0, 1]
    for leaf in range(1, 8):
        given = given + kb[leaf, 1]
    own = own + jnp.concatenate([jnp.where(g == other, given, 0.0) for other in range(8)], axis=1)
    share(own, 0)
    accf[...] = jnp.concatenate([kb[leaf, 2] for leaf in range(8)], axis=1)
    accl[...] = jnp.concatenate([kb[leaf, 3] for leaf in range(8)], axis=1)
    for turn in range(2):
        @pl.when(first_panel if turn == 0 else last_panel)
        def _(turn=turn):
            yin[turn] = jnp.zeros((16, SEP // 2), BF16)

    wait(gs.at[:, pl.ds(0, 7)], rsem.at[X_SINV])
    own_sinv.wait()
    stot[...] = solve(0)

    @pl.when(p > 0)
    def _():
        wait(yin.at[0], rsem.at[X_YF])
        face = unfold(yin[0]).astype(BF16)
        arrived(T_F)
        share(-scatter(leafwise(face, T_F)), 1)
        arrived(D_FF)
        accf[...] += leafwise(face, D_FF)

        @pl.when(p < 3)
        def _():
            arrived(D_F)
            accl[...] += leafwise(face, D_F)

        stot[...] += solve(1)

    @pl.when(p < 3)
    def _():
        arrived(O_F)
        yout[0] = fold(accl[...] - leafwise(gather(stot[...]).astype(BF16), O_F))
        send(yout.at[0], yin.at[0], X_YF, (p + 1, front))

    @pl.when(p < 3)
    def _():
        wait(yin.at[1], rsem.at[X_YB])
        face = unfold(yin[1]).astype(BF16)
        arrived(T_B)
        share(-scatter(leafwise(face, T_B)), 2)

        @pl.when(p > 0)
        def _():
            arrived(D_B)
            accf[...] += leafwise(face, D_B)

        stot[...] += solve(2)

    picked = gather(stot[...])

    @pl.when(p > 0)
    def _():
        arrived(O_B)
        yout[1] = fold(accf[...] - leafwise(picked.astype(BF16), O_B))
        send(yout.at[1], yin.at[1], X_YB, (p - 1, front))

    low_face, high_face = unfold(yin[0]), unfold(yin[1])
    own_sep = sbuf[0, g]
    own_sep = own_sep + jnp.where(p > 0, sbuf[1, g], 0.0)
    own_sep = own_sep + jnp.where(p < 3, sbuf[2, g], 0.0)
    for leaf in range(8):
        cols = slice(leaf * FACE, (leaf + 1) * FACE)
        fstage[leaf, 0] = picked[:, cols]
        fstage[leaf, 1] = low_face[:, cols]
        fstage[leaf, 2] = high_face[:, cols]
        fstage[leaf, 3] = own_sep
    for k in range(1, 8):
        other, device = z_peer(k)
        send(fstage.at[other], fk.at[z], X_FINAL, device)
    fk[z] = fstage[z]
    wait(fk.at[pl.ds(0, 7)], rsem.at[X_FINAL])
    sep_ref[...] = jnp.concatenate([fk[other, 3:4] for other in range(8)], axis=0)

    def rows_of(item):
        tops = [fk[other, item][:4] for other in range(8)]
        bottoms = [fk[other, item][4:] for other in range(8)]
        return jnp.concatenate(tops, axis=0), jnp.concatenate(bottoms, axis=0)

    pick_re, pick_im = rows_of(0)
    doubled = jnp.concatenate(
        [jnp.concatenate([pick_re, -pick_im], axis=1), jnp.concatenate([pick_im, pick_re], axis=1)], axis=0
    ).astype(BF16)
    side = rhs_ref[...].reshape(64, CELLS) - lax.dot_general(doubled, link, NT, preferred_element_type=F32)
    add_low = jnp.concatenate(rows_of(1), axis=0)
    add_high = jnp.concatenate(rows_of(2), axis=0)
    side = jnp.concatenate(
        [side[:, :FACE] + add_low, side[:, FACE : CELLS - FACE], side[:, CELLS - FACE :] + add_high], axis=1
    ).astype(BF16)
    for block in range(5):
        cols = pl.ds(block * BLOCK, BLOCK)
        real = dot(side, inv[0, :, cols])
        imag = dot(side, inv[1, :, cols])
        out_ref[0, :, cols] = real[:32] - imag[32:]
        out_ref[1, :, cols] = real[32:] + imag[:32]

    def left(ref, which):
        wait(ref, ssem.at[which])

    left(gs.at[:, pl.ds(0, 7)], X_SINV)
    left(gi.at[pl.ds(0, 7)], X_IDX)
    left(kb.at[pl.ds(0, 7)], X_BASE)
    left(fk.at[pl.ds(0, 7)], X_FINAL)
    for slot in range(7):
        @pl.when(needed[slot])
        def _(slot=slot):
            left(gm.at[slot, pl.ds(0, 7)], X_MAT + slot)
    for turn, used in ((0, None), (1, p > 0), (2, p < 3)):
        def both_left(turn=turn):
            left(pbuf.at[turn, pl.ds(0, 7)], X_PART + turn)
            left(sbuf.at[turn, pl.ds(0, 7)], X_SOL + turn)
        if used is None:
            both_left()
        else:
            pl.when(used)(both_left)

    @pl.when(p < 3)
    def _():
        left(yin.at[0], X_YF)

    @pl.when(p > 0)
    def _():
        left(yin.at[1], X_YB)


def local(leaf_rhs, sep_rhs, leaf_inverse, coupling, sep_index, sep_inverse):
    z = lax.rem(lax.axis_index("front") // 2, 8)
    t = sep_index[0, 0]
    order = ((t // 256) * 2 + (t // 16) % 2) * 128 + ((t // 32) % 8) * 16 + t % 16
    index = jnp.broadcast_to(order[None, :], (8, FACE))
    sinv = sep_inverse[0].reshape(2, 4, 8, 2, 16, 16).transpose(0, 5, 1, 3, 2, 4).reshape(2, 16, SEP)
    lane = lax.broadcasted_iota(jnp.int32, (1, 1, FACE), 2)
    given = jnp.where(lane // 16 == z, jnp.tile(sep_rhs[0], (1, 1, 8)), 0.0)
    vmem = pl.BlockSpec(memory_space=pltpu.VMEM)
    hbm = pl.BlockSpec(memory_space=pl.ANY)
    leaf, sep = pl.pallas_call(
        kernel,
        out_shape=(jax.ShapeDtypeStruct((2, 32, CELLS), F32), jax.ShapeDtypeStruct((8, 8, FACE), F32)),
        in_specs=[vmem, vmem, hbm, vmem, vmem, hbm],
        out_specs=(vmem, vmem),
        scratch_shapes=[
            pltpu.VMEM((2, CELLS, CELLS), BF16),
            pltpu.VMEM((CELLS, 2 * FACE), BF16),
            pltpu.VMEM((7, 8, FACE, 2 * FACE), BF16),
            pltpu.VMEM((2, 8, 16, SEP), BF16),
            pltpu.VMEM((8, 8, FACE), jnp.int32),
            pltpu.VMEM((SEP, SEP), BF16),
            pltpu.VMEM((8, 4, 8, FACE), F32),
            pltpu.VMEM((8, 4, 8, FACE), F32),
            pltpu.VMEM((3, 8, 16, SEP // 2), BF16),
            pltpu.VMEM((3, 8, 8, FACE), F32),
            pltpu.VMEM((2, 16, SEP // 2), BF16),
            pltpu.VMEM((2, 16, SEP // 2), BF16),
            pltpu.VMEM((8, 4, 8, FACE), F32),
            pltpu.VMEM((8, 4, 8, FACE), F32),
            pltpu.VMEM((8, SEP), F32),
            pltpu.VMEM((8, SEP), F32),
            pltpu.VMEM((8, SEP), F32),
            pltpu.SemaphoreType.DMA((6,)),
            pltpu.SemaphoreType.DMA((X_COUNT,)),
            pltpu.SemaphoreType.DMA((X_COUNT,)),
        ],
        compiler_params=pltpu.CompilerParams(
            collective_id=0, has_side_effects=True, vmem_limit_bytes=48 * 2**20
        ),
    )(leaf_rhs[0, 0], given, leaf_inverse[0, 0], coupling[0, 0], index, sinv)
    mine = lax.dynamic_slice_in_dim(sep, z * 16, 16, axis=2)
    sep_out = mine.reshape(8, 2, 4, 16).transpose(1, 0, 2, 3).reshape(2, 32, 16)
    return leaf[None, None], sep_out[None]


def solution(mesh):
    in_specs = (
        P("panel", "front", None, None, None),
        P("panel", None, None, "front"),
        P("panel", "front", None, None, None),
        P("panel", "front", None, None, None),
        P("panel", "front", None),
        P("panel", None, None, "front"),
    )
    out_specs = (P("panel", "front", None, None, None), P("panel", None, None, "front"))
    return jax.shard_map(local, mesh=mesh, in_specs=in_specs, out_specs=out_specs, check_vma=False)
```

```python
import jax
import jax.numpy as jnp
from jax import lax
from jax.experimental import pallas as pl
from jax.experimental.pallas import tpu as pltpu
from jax.sharding import PartitionSpec as P

MESH = pl.DeviceIdType.MESH
F32 = jnp.float32
BF16 = jnp.bfloat16
FACE = 128
CELLS = 1280
SEP = 1024
BLOCK = 256
NT = (((1,), (1,)), ((), ()))
TN = (((0,), (0,)), ((), ()))

S_T, S_O, S_D, S_O2, S_T2, S_D2, S_DFF, R_SINV = range(8)
FIRST_SET, SECOND_SET = (S_O, S_T, S_D), (S_O2, S_T2, S_D2, S_DFF)
X_UP, X_DOWN, X_IDX, X_BASE, X_T, X_T2, X_PART, X_SOL, X_Y, X_FINAL, X_COUNT = 0, 1, 2, 3, 4, 5, 6, 9, 12, 15, 16


def dot(a, b):
    return jnp.dot(a, b, preferred_element_type=F32)


def kernel(rhs_hbm, bs_hbm, inv_hbm, cc_hbm, idx_hbm, sinv_hbm, out_ref, sep_ref,
           rhs, bs, inv, cc, idx, w, tst, gm, gs, gi, pto, ptb, pta, ptz, stage, kb, pbuf, pout, sbuf, yout, yin,
           bst, fstage, fk, acca, accb, stot, lsem, ssem, rsem, rs, rr):
    p = lax.axis_index("panel")
    front = lax.axis_index("front")
    x, z, c = front // 16, lax.rem(front // 2, 8), lax.rem(front, 2)
    g = x * 2 + c
    middle = (p > 0) & (p < 3)
    ahead = jnp.where(p < 3, p + 1, 2)
    turn_ahead = jnp.where(p < 3, 1, 2)

    def z_peer(k):
        other = lax.rem(z + k, 8)
        return other, (p, (x * 8 + other) * 2 + c)

    def g_peer(k, panel):
        other = lax.rem(g + k, 8)
        return panel, ((other // 2) * 8 + z) * 2 + lax.rem(other, 2)

    def load(src, dst, number):
        copy = pltpu.make_async_copy(src, dst, lsem.at[number])
        copy.start()
        return copy

    load_sinv = load(sinv_hbm, gs.at[:, z], 0)
    load_idx = load(idx_hbm, idx, 1)
    load_cc = load(cc_hbm, cc, 2)
    load_inv = []
    for block in range(5):
        rows = pl.ds(block * BLOCK, BLOCK)
        load_inv.append(load(inv_hbm.at[:, rows], inv.at[:, rows], 3 + block))
        if block == 0:
            load_rhs = load(rhs_hbm, rhs, 8)
    load_bs = load(bs_hbm, bs, 9)

    barrier = pltpu.get_barrier_semaphore()

    def greet(device):
        pl.semaphore_signal(barrier, inc=1, device_id=device, device_id_type=MESH)

    for k in range(1, 8):
        greet(z_peer(k)[1])
        greet(g_peer(k, p))

    @pl.when(p > 0)
    def _():
        for k in range(8):
            greet(g_peer(k, p - 1))

    @pl.when(p < 3)
    def _():
        for k in range(8):
            greet(g_peer(k, p + 1))

    bst[...] = jnp.zeros((2, FACE, 32), F32)
    pl.semaphore_wait(barrier, 14 + jnp.where(p > 0, 8, 0) + jnp.where(p < 3, 8, 0))

    def send(src, dst, which, device):
        pltpu.make_async_remote_copy(
            src_ref=src, dst_ref=dst, send_sem=ssem.at[which], recv_sem=rsem.at[which], device_id=device, device_id_type=MESH
        ).start()

    def wait(ref, sem):
        pltpu.make_async_copy(ref, ref, sem).wait()

    def block_of(slot, owner):
        return gs.at[:, owner] if slot == R_SINV else gm.at[slot, owner]

    def ring(slot, step):
        for way, steps in ((0, 4), (1, 3)):
            if step < steps:
                if step > 0:
                    wait(block_of(slot, 0), rr.at[slot, way, step - 1])
                owner = lax.rem(z + (8 - step if way == 0 else step), 8)
                pltpu.make_async_remote_copy(
                    src_ref=block_of(slot, owner), dst_ref=block_of(slot, owner), send_sem=rs.at[slot, way, step],
                    recv_sem=rr.at[slot, way, step], device_id=z_peer(1 if way == 0 else 7)[1], device_id_type=MESH
                ).start()

    def ring_end(slot):
        wait(block_of(slot, 0), rr.at[slot, 0, 3])
        wait(block_of(slot, 0), rr.at[slot, 1, 2])

    def ring_left(slot):
        for way, steps in ((0, 4), (1, 3)):
            for step in range(steps):
                wait(block_of(slot, 0), rs.at[slot, way, step])

    def first_set(step):
        ring(S_O, step)
        ring(S_T, step)

        @pl.when(p > 0)
        def _():
            ring(S_D, step)

    def second_set(step):
        for slot in SECOND_SET:
            ring(slot, step)

    load_sinv.wait()
    ring(R_SINV, 0)
    load_idx.wait()
    own_index = jnp.broadcast_to(idx[...], (8, FACE))
    gi[z, 0] = own_index

    @pl.when(p == 0)
    def _():
        gi[z, 2] = own_index

    @pl.when(p == 3)
    def _():
        gi[z, 1] = own_index

    @pl.when(p < 3)
    def _():
        send(gi.at[z, 0], gi.at[z, 2], X_UP, (p + 1, front))

    @pl.when(p > 0)
    def _():
        send(gi.at[z, 0], gi.at[z, 1], X_DOWN, (p - 1, front))

    load_cc.wait()
    load_rhs.wait()
    flat = rhs[...].reshape(64, CELLS).astype(BF16)
    towards = jnp.zeros((64, 2 * FACE), F32)
    faces = [jnp.zeros((64, 2 * FACE), F32) for _ in range(2)]
    link = jnp.concatenate([cc[0], cc[1]], axis=1)
    starts = (0, CELLS - FACE)
    for block in range(5):
        rows = pl.ds(block * BLOCK, BLOCK)
        load_inv[block].wait()
        real = dot(inv[0, rows], link)
        imag = dot(inv[1, rows], link)
        part = jnp.concatenate(
            [real[:, :FACE] - imag[:, FACE:], real[:, FACE:] + imag[:, :FACE]], axis=1
        ).astype(BF16)
        w[rows] = part
        some = flat[:, block * BLOCK : (block + 1) * BLOCK]
        towards = towards + dot(some, part)
        for side, start in enumerate(starts):
            cols = pl.ds(start, FACE)
            both = jnp.concatenate([inv[0, rows, cols], inv[1, rows, cols]], axis=1)
            faces[side] = faces[side] + dot(some, both)
        if block == 0:
            tst[0] = part[:FACE]

            @pl.when(p > 0)
            def _():
                send(tst.at[0], gm.at[S_T, z], X_T, (p - 1, front))
        if block == 1:
            ring(R_SINV, 1)

            @pl.when(p > 0)
            def _():
                wait(gi.at[0, 0], rsem.at[X_UP])

            @pl.when(p < 3)
            def _():
                wait(gi.at[0, 0], rsem.at[X_DOWN])

            for k in range(1, 8):
                send(gi.at[z], gi.at[z], X_IDX, z_peer(k)[1])
        if block == 3:
            ring(R_SINV, 2)
    tst[1] = w[pl.ds(CELLS - FACE, FACE)]

    def combine(value):
        return jnp.concatenate(
            [value[:32, :FACE] - value[32:, FACE:], value[32:, :FACE] + value[:32, FACE:]], axis=0
        )

    load_bs.wait()
    place = pl.ds(pl.multiple_of(lax.rem(z, 4) * 32 + c * 16, 16), 16)
    for part in range(2):
        bst[part, place] = bs[part]
    given = jnp.concatenate([jnp.transpose(bst[0]), jnp.transpose(bst[1])], axis=0)
    face_first, face_last = combine(faces[0]), combine(faces[1])
    pieces = [combine(towards), given, jnp.where(p < 3, face_last, face_first), face_first]
    for other in range(8):
        for item, value in enumerate(pieces):
            stage[other, item] = jnp.concatenate(
                [value[4 * other : 4 * other + 4], value[32 + 4 * other : 36 + 4 * other]], axis=0
            )
    for k in range(1, 8):
        other, device = z_peer(k)
        send(stage.at[other], kb.at[z], X_BASE, device)
    kb[z] = stage[z]

    @pl.when(p == 2)
    def _():
        send(tst.at[1], gm.at[S_T, z], X_T, (3, front))

    @pl.when(p < 2)
    def _():
        send(tst.at[1], gm.at[S_T2, z], X_T2, (p + 1, front))

    ring(R_SINV, 3)
    outs = []
    for side, start in enumerate(starts):
        total = jnp.zeros((2 * FACE, 2 * FACE), F32)
        for block in range(5):
            rows, cols = pl.ds(block * BLOCK, BLOCK), pl.ds(start, FACE)
            both = jnp.concatenate([inv[0, rows, cols], inv[1, rows, cols]], axis=1)
            total = total + lax.dot_general(
                link[block * BLOCK : (block + 1) * BLOCK], both, TN, preferred_element_type=F32
            )
        outs.append(
            jnp.concatenate(
                [total[:FACE, :FACE] - total[FACE:, FACE:], total[:FACE, FACE:] + total[FACE:, :FACE]], axis=1
            )
        )
    gm[S_O, z] = jnp.where(p < 3, outs[1], outs[0]).astype(BF16)
    gm[S_O2, z] = outs[0].astype(BF16)
    low, high = pl.ds(0, FACE), pl.ds(CELLS - FACE, FACE)
    d_ff = jnp.concatenate([inv[0, low, low], inv[1, low, low]], axis=1)
    gm[S_DFF, z] = d_ff
    gm[S_D2, z] = jnp.concatenate([inv[0, high, low], inv[1, high, low]], axis=1)
    gm[S_D, z] = jnp.where(p < 3, jnp.concatenate([inv[0, low, high], inv[1, low, high]], axis=1), d_ff)
    wait(gm.at[S_T, 0], rsem.at[X_T])
    first_set(0)

    unknown = lax.broadcasted_iota(jnp.int32, (SEP, FACE), 0)

    def select(dst, item, by_row=False):
        for leaf in range(8):
            row = gi[leaf, item][0:1, :]
            if by_row:
                row = ((row >> 8) * 2 + ((row >> 4) & 1)) * 128 + ((row >> 5) & 7) * 16 + (row & 15)
            dst[:, leaf * FACE : (leaf + 1) * FACE] = jnp.where(unknown == row, 1.0, 0.0).astype(BF16)

    wait(gi.at[pl.ds(0, 7)], rsem.at[X_IDX])
    select(ptb, 0)

    sign = jnp.where(lax.broadcasted_iota(jnp.int32, (8, SEP), 0) < 4, -1.0, 1.0)

    def leafwise(vector, slot):
        parts = [dot(vector[:, leaf * FACE : (leaf + 1) * FACE], gm[slot, leaf]) for leaf in range(8)]
        direct = jnp.concatenate([v[:, :FACE] for v in parts], axis=1)
        crossed = jnp.concatenate([v[:, FACE:] for v in parts], axis=1)
        return direct + sign * jnp.roll(crossed, 4, axis=0)

    def fold(value):
        half = value.shape[1] // 2
        return jnp.concatenate([value[:, :half], value[:, half:]], axis=0).astype(BF16)

    def unfold(value):
        value = value.astype(F32)
        return jnp.concatenate([value[:8], value[8:]], axis=1)

    def scatter(value, matrix):
        return lax.dot_general(value.astype(BF16), matrix[...], NT, preferred_element_type=F32)

    def gather(value):
        return dot(value.astype(BF16), pto[...])

    def solve(turn, arrived, before, meanwhile):
        before()
        wait(pbuf.at[turn, pl.ds(0, arrived)], rsem.at[X_PART + turn])
        total = pbuf[turn, 0].astype(F32)
        for other in range(1, 8):
            total = total + pbuf[turn, other].astype(F32)
        reduced = unfold(total).astype(BF16)
        both = lax.dot_general(reduced, gs[...].reshape(2 * FACE, SEP), NT, preferred_element_type=F32)
        mine = both[:, :FACE] + sign[:, :FACE] * jnp.roll(both[:, FACE:], 4, axis=0)
        sbuf[turn, g] = mine
        for k in range(1, 8):
            send(sbuf.at[turn, g], sbuf.at[turn, g], X_SOL + turn, g_peer(k, p))
        meanwhile()
        wait(sbuf.at[turn, pl.ds(0, 7)], rsem.at[X_SOL + turn])
        return jnp.concatenate([sbuf[turn, other] for other in range(8)], axis=1)

    def onward(face, matrix, slot, which, turn, panel):
        face_low = face.astype(BF16)
        pout[which] = fold(-scatter(leafwise(face_low, slot), matrix))
        for k in range(8):
            send(pout.at[which], pbuf.at[turn, g], X_PART + turn, g_peer(k, panel))
        yout[which] = fold(face)
        send(yout.at[which], yin.at[turn], X_Y + turn, (panel, front))

    wait(kb.at[pl.ds(0, 7)], rsem.at[X_BASE])
    own = -scatter(jnp.concatenate([kb[leaf, 0] for leaf in range(8)], axis=1), ptb)
    given_low = (kb[0, 1] + kb[1, 1]) + (kb[2, 1] + kb[3, 1])
    given_high = (kb[4, 1] + kb[5, 1]) + (kb[6, 1] + kb[7, 1])
    own = own + jnp.concatenate(
        [jnp.where(x == other // 2, given_low if other % 2 == 0 else given_high, 0.0) for other in range(8)], axis=1
    )
    pbuf[0, g] = fold(own)
    for k in range(1, 8):
        send(pbuf.at[0, g], pbuf.at[0, g], X_PART, g_peer(k, p))
    acca[...] = jnp.concatenate([kb[leaf, 2] for leaf in range(8)], axis=1)
    accb[...] = jnp.concatenate([kb[leaf, 3] for leaf in range(8)], axis=1)

    @pl.when(p == 0)
    def _():
        yin[1] = jnp.zeros((16, SEP // 2), BF16)

    @pl.when(p == 3)
    def _():
        yin[2] = jnp.zeros((16, SEP // 2), BF16)

    def base_before():
        select(pto, 0, by_row=True)
        first_set(1)
        ring_end(R_SINV)

    def base_meanwhile():
        @pl.when(p < 3)
        def _():
            select(pta, 1)

        @pl.when(p == 3)
        def _():
            select(pta, 2)

        first_set(2)

    stot[...] = solve(0, 7, base_before, base_meanwhile)
    first_set(3)

    @pl.when(middle)
    def _():
        wait(gm.at[S_T2, 0], rsem.at[X_T2])
        second_set(0)
        second_set(1)

    @pl.when(p > 0)
    def _():
        def meanwhile():
            wait(yin.at[1], rsem.at[X_Y + 1])
            ring_end(S_D)
            acca[...] += leafwise(unfold(yin[1]).astype(BF16), S_D)

        stot[...] += solve(1, 8, lambda: None, meanwhile)

    ring_end(S_O)
    ring_end(S_T)
    onward(acca[...] - leafwise(gather(stot[...]).astype(BF16), S_O), pta, S_T, 0, turn_ahead, ahead)

    @pl.when(middle)
    def _():
        select(ptz, 2)
        second_set(2)
        second_set(3)
        for slot in SECOND_SET:
            ring_end(slot)
        accb[...] += leafwise(unfold(yin[1]).astype(BF16), S_DFF)

    @pl.when(p < 3)
    def _():
        def meanwhile():
            wait(yin.at[2], rsem.at[X_Y + 2])

            @pl.when(p > 0)
            def _():
                accb[...] += leafwise(unfold(yin[2]).astype(BF16), S_D2)

        stot[...] += solve(2, 8, lambda: None, meanwhile)

    picked = gather(stot[...])

    @pl.when(middle)
    def _():
        onward(accb[...] - leafwise(picked.astype(BF16), S_O2), ptz, S_T2, 1, 2, p - 1)

    low_face, high_face = unfold(yin[1]), unfold(yin[2])
    own_sep = sbuf[0, g]
    own_sep = own_sep + jnp.where(p > 0, sbuf[1, g], 0.0)
    own_sep = own_sep + jnp.where(p < 3, sbuf[2, g], 0.0)
    for leaf in range(8):
        cols = slice(leaf * FACE, (leaf + 1) * FACE)
        fstage[leaf, 0] = picked[:, cols]
        fstage[leaf, 1] = low_face[:, cols]
        fstage[leaf, 2] = high_face[:, cols]
        fstage[leaf, 3] = own_sep
    for k in range(1, 8):
        other, device = z_peer(k)
        send(fstage.at[other], fk.at[z], X_FINAL, device)
    fk[z] = fstage[z]
    wait(fk.at[pl.ds(0, 7)], rsem.at[X_FINAL])

    def rows_of(item):
        tops = [fk[other, item][:4] for other in range(8)]
        bottoms = [fk[other, item][4:] for other in range(8)]
        return jnp.concatenate(tops, axis=0), jnp.concatenate(bottoms, axis=0)

    for part, value in enumerate(rows_of(3)):
        bst[part] = jnp.transpose(value)
        sep_ref[part] = bst[part, pl.ds(pl.multiple_of(z * 16, 16), 16)]
    pick_re, pick_im = rows_of(0)
    doubled = jnp.concatenate(
        [jnp.concatenate([pick_re, -pick_im], axis=1), jnp.concatenate([pick_im, pick_re], axis=1)], axis=0
    ).astype(BF16)
    side = rhs[...].reshape(64, CELLS) - lax.dot_general(doubled, link, NT, preferred_element_type=F32)
    add_low = jnp.concatenate(rows_of(1), axis=0)
    add_high = jnp.concatenate(rows_of(2), axis=0)
    side = jnp.concatenate(
        [side[:, :FACE] + add_low, side[:, FACE : CELLS - FACE], side[:, CELLS - FACE :] + add_high], axis=1
    ).astype(BF16)
    for block in range(5):
        cols = pl.ds(block * BLOCK, BLOCK)
        real = dot(side, inv[0, :, cols])
        imag = dot(side, inv[1, :, cols])
        out_ref[0, :, cols] = real[:32] - imag[32:]
        out_ref[1, :, cols] = real[32:] + imag[:32]

    ring_left(R_SINV)
    ring_left(S_O)
    ring_left(S_T)
    wait(gi.at[pl.ds(0, 7)], ssem.at[X_IDX])
    wait(kb.at[pl.ds(0, 7)], ssem.at[X_BASE])
    wait(fk.at[pl.ds(0, 7)], ssem.at[X_FINAL])
    wait(pbuf.at[0, pl.ds(0, 7)], ssem.at[X_PART])
    wait(sbuf.at[0, pl.ds(0, 7)], ssem.at[X_SOL])

    @pl.when(p > 0)
    def _():
        ring_left(S_D)
        wait(gi.at[0, 0], ssem.at[X_DOWN])
        wait(pbuf.at[2], ssem.at[X_PART + 2])
        wait(sbuf.at[1, pl.ds(0, 7)], ssem.at[X_SOL + 1])
        wait(yin.at[2], ssem.at[X_Y + 2])

    @pl.when(p < 3)
    def _():
        wait(gi.at[0, 0], ssem.at[X_UP])
        wait(pbuf.at[1], ssem.at[X_PART + 1])
        wait(sbuf.at[2, pl.ds(0, 7)], ssem.at[X_SOL + 2])
        wait(yin.at[1], ssem.at[X_Y + 1])

    @pl.when((p == 1) | (p == 3))
    def _():
        wait(tst.at[0], ssem.at[X_T])

    @pl.when(p == 2)
    def _():
        wait(tst, ssem.at[X_T])

    @pl.when(p < 2)
    def _():
        wait(tst.at[1], ssem.at[X_T2])

    @pl.when(middle)
    def _():
        for slot in SECOND_SET:
            ring_left(slot)


def local(leaf_rhs, sep_rhs, leaf_inverse, coupling, sep_index, sep_inverse):
    vmem = pl.BlockSpec(memory_space=pltpu.VMEM)
    hbm = pl.BlockSpec(memory_space=pl.ANY)
    leaf, sep = pl.pallas_call(
        kernel,
        out_shape=(jax.ShapeDtypeStruct((2, 32, CELLS), F32), jax.ShapeDtypeStruct((2, 16, 32), F32)),
        in_specs=[hbm] * 6,
        out_specs=(vmem, vmem),
        scratch_shapes=[
            pltpu.VMEM((2, 32, CELLS), F32),
            pltpu.VMEM((2, 16, 32), F32),
            pltpu.VMEM((2, CELLS, CELLS), BF16),
            pltpu.VMEM((2, CELLS, FACE), BF16),
            pltpu.VMEM((1, FACE), jnp.int32),
            pltpu.VMEM((CELLS, 2 * FACE), BF16),
            pltpu.VMEM((2, FACE, 2 * FACE), BF16),
            pltpu.VMEM((7, 8, FACE, 2 * FACE), BF16),
            pltpu.VMEM((2, 8, 16, SEP), BF16),
            pltpu.VMEM((8, 3, 8, FACE), jnp.int32),
            pltpu.VMEM((SEP, SEP), BF16),
            pltpu.VMEM((SEP, SEP), BF16),
            pltpu.VMEM((SEP, SEP), BF16),
            pltpu.VMEM((SEP, SEP), BF16),
            pltpu.VMEM((8, 4, 8, FACE), F32),
            pltpu.VMEM((8, 4, 8, FACE), F32),
            pltpu.VMEM((3, 8, 16, SEP // 2), BF16),
            pltpu.VMEM((2, 16, SEP // 2), BF16),
            pltpu.VMEM((3, 8, 8, FACE), F32),
            pltpu.VMEM((2, 16, SEP // 2), BF16),
            pltpu.VMEM((3, 16, SEP // 2), BF16),
            pltpu.VMEM((2, FACE, 32), F32),
            pltpu.VMEM((8, 4, 8, FACE), F32),
            pltpu.VMEM((8, 4, 8, FACE), F32),
            pltpu.VMEM((8, SEP), F32),
            pltpu.VMEM((8, SEP), F32),
            pltpu.VMEM((8, SEP), F32),
            pltpu.SemaphoreType.DMA((10,)),
            pltpu.SemaphoreType.DMA((X_COUNT,)),
            pltpu.SemaphoreType.DMA((X_COUNT,)),
            pltpu.SemaphoreType.DMA((8, 2, 4)),
            pltpu.SemaphoreType.DMA((8, 2, 4)),
        ],
        compiler_params=pltpu.CompilerParams(
            collective_id=0, has_side_effects=True, vmem_limit_bytes=56 * 2**20
        ),
    )(
        leaf_rhs[0, 0], sep_rhs[0].transpose(0, 2, 1), leaf_inverse[0, 0], coupling[0, 0], sep_index[0],
        sep_inverse[0].transpose(0, 2, 1)
    )
    return leaf[None, None], sep.transpose(0, 2, 1)[None]


def solution(mesh):
    in_specs = (
        P("panel", "front", None, None, None),
        P("panel", None, None, "front"),
        P("panel", "front", None, None, None),
        P("panel", "front", None, None, None),
        P("panel", "front", None),
        P("panel", None, None, "front"),
    )
    out_specs = (P("panel", "front", None, None, None), P("panel", None, None, "front"))
    return jax.shard_map(local, mesh=mesh, in_specs=in_specs, out_specs=out_specs, check_vma=False)
```

```python
import jax
import jax.numpy as jnp
from jax import lax
from jax.experimental import pallas as pl
from jax.experimental.pallas import tpu as pltpu
from jax.sharding import PartitionSpec as P

MESH = pl.DeviceIdType.MESH
F32 = jnp.float32
BF16 = jnp.bfloat16
FACE = 128
CELLS = 1280
SEP = 1024
BLOCK = 256
NT = (((1,), (1,)), ((), ()))
TN = (((0,), (0,)), ((), ()))

S_T, S_O, S_D, S_O2, S_T2, S_D2, S_DFF, R_SINV = range(8)
Z_ORDER, G_ORDER = (4, 3, 5, 2, 6, 1, 7), (4, 5, 2, 6, 3, 7, 1, 0)
FIRST_SET, SECOND_SET = (S_O, S_T, S_D), (S_O2, S_T2, S_D2, S_DFF)
X_UP, X_DOWN, X_IDX, X_BASE, X_T, X_T2, X_PART, X_SOL, X_Y, X_FACES, X_FINAL, X_IDX2, X_BASE2, X_COUNT = 0, 1, 2, 3, 4, 5, 6, 9, 12, 15, 16, 17, 18, 19


def dot(a, b):
    return jnp.dot(a, b, preferred_element_type=F32)


def kernel(rhs_hbm, bs_hbm, inv_hbm, cc_hbm, idx_hbm, sinv_hbm, out_ref, sep_ref,
           rhs, bs, inv, cc, idx, w, tst, gm, gs, gi, pto, ptb, pta, ptz, stage, kb, pbuf, pout, sbuf, yout, yin,
           bst, hstage, hk, fstage, fk, acca, accb, stot, lsem, ssem, rsem, rs, rr):
    p = lax.axis_index("panel")
    front = lax.axis_index("front")
    x, z, c = front // 16, lax.rem(front // 2, 8), lax.rem(front, 2)
    g = x * 2 + c
    middle = (p > 0) & (p < 3)
    ahead = jnp.where(p < 3, p + 1, 2)
    turn_ahead = jnp.where(p < 3, 1, 2)

    def z_peer(k):
        other = lax.rem(z + k, 8)
        return other, (p, (x * 8 + other) * 2 + c)

    def g_peer(k, panel):
        return panel, (lax.rem(x + k // 2, 4) * 8 + z) * 2 + lax.rem(c + k % 2, 2)

    def load(src, dst, number):
        copy = pltpu.make_async_copy(src, dst, lsem.at[number])
        copy.start()
        return copy

    load_sinv = load(sinv_hbm, gs.at[:, z], 0)
    load_idx = load(idx_hbm, idx, 1)
    load_cc = load(cc_hbm, cc, 2)
    load_inv = []
    for block in range(5):
        rows = pl.ds(block * BLOCK, BLOCK)
        load_inv.append(load(inv_hbm.at[:, rows], inv.at[:, rows], 3 + block))
        if block == 0:
            load_rhs = load(rhs_hbm, rhs, 8)
    load_bs = load(bs_hbm, bs, 9)

    barrier = pltpu.get_barrier_semaphore()

    def greet(device):
        pl.semaphore_signal(barrier, inc=1, device_id=device, device_id_type=MESH)

    for k in range(1, 8):
        greet(z_peer(k)[1])
        greet(g_peer(k, p))

    @pl.when(p > 0)
    def _():
        for k in range(8):
            greet(g_peer(k, p - 1))

    @pl.when(p < 3)
    def _():
        for k in range(8):
            greet(g_peer(k, p + 1))

    bst[...] = jnp.zeros((2, FACE, 32), F32)

    def send(src, dst, which, device):
        pltpu.make_async_remote_copy(
            src_ref=src, dst_ref=dst, send_sem=ssem.at[which], recv_sem=rsem.at[which], device_id=device, device_id_type=MESH
        ).start()

    def wait(ref, sem):
        pltpu.make_async_copy(ref, ref, sem).wait()

    onto = jnp.where(c == 0, 1, 7)

    def block_of(slot, owner):
        return gs.at[:, owner] if slot == R_SINV else gm.at[slot, owner]

    def ring(slot, step):
        for way, steps in ((0, 4), (1, 3)):
            if step < steps:
                if step > 0:
                    wait(block_of(slot, 0), rr.at[slot, way, step - 1])
                owner = lax.rem(z + step * (8 - onto if way == 0 else onto), 8)
                pltpu.make_async_remote_copy(
                    src_ref=block_of(slot, owner), dst_ref=block_of(slot, owner), send_sem=rs.at[slot, way, step],
                    recv_sem=rr.at[slot, way, step], device_id=z_peer(onto if way == 0 else 8 - onto)[1], device_id_type=MESH
                ).start()

    def ring_end(slot):
        wait(block_of(slot, 0), rr.at[slot, 0, 3])
        wait(block_of(slot, 0), rr.at[slot, 1, 2])

    def ring_left(slot):
        for way, steps in ((0, 4), (1, 3)):
            for step in range(steps):
                wait(block_of(slot, 0), rs.at[slot, way, step])

    def first_set(step):
        ring(S_T, step)
        ring(S_O, step)

        @pl.when(p > 0)
        def _():
            ring(S_D, step)

    def second_set(step):
        for slot in SECOND_SET:
            ring(slot, step)

    def begin():
        pl.semaphore_wait(barrier, 14 + jnp.where(p > 0, 8, 0) + jnp.where(p < 3, 8, 0))
        load_sinv.wait()
        ring(R_SINV, 0)
        load_idx.wait()
        own_index = idx[...]
        gi[z, 0] = own_index
        for k in Z_ORDER:
            send(gi.at[z, 0], gi.at[z, 0], X_IDX, z_peer(k)[1])

        @pl.when(p == 0)
        def _():
            gi[z, 2] = own_index

        @pl.when(p == 3)
        def _():
            gi[z, 1] = own_index

        @pl.when(p < 3)
        def _():
            send(gi.at[z, 0], gi.at[z, 2], X_UP, (p + 1, front))

        @pl.when(p > 0)
        def _():
            send(gi.at[z, 0], gi.at[z, 1], X_DOWN, (p - 1, front))

    load_cc.wait()
    load_rhs.wait()
    flat = rhs[...].reshape(64, CELLS).astype(BF16)
    towards = jnp.zeros((64, 2 * FACE), F32)
    faces = [jnp.zeros((64, 2 * FACE), F32) for _ in range(2)]
    link = jnp.concatenate([cc[0], cc[1]], axis=1)
    starts = (0, CELLS - FACE)
    for block in range(5):
        rows = pl.ds(block * BLOCK, BLOCK)
        load_inv[block].wait()
        real = dot(inv[0, rows], link)
        imag = dot(inv[1, rows], link)
        part = jnp.concatenate(
            [real[:, :FACE] - imag[:, FACE:], real[:, FACE:] + imag[:, :FACE]], axis=1
        ).astype(BF16)
        w[rows] = part
        some = flat[:, block * BLOCK : (block + 1) * BLOCK]
        towards = towards + dot(some, part)
        for side, start in enumerate(starts):
            cols = pl.ds(start, FACE)
            both = jnp.concatenate([inv[0, rows, cols], inv[1, rows, cols]], axis=1)
            faces[side] = faces[side] + dot(some, both)
        if block == 0:
            tst[0] = part[:FACE]
        if block == 1:
            begin()

            @pl.when(p > 0)
            def _():
                send(tst.at[0], gm.at[S_T, z], X_T, (p - 1, front))
        if block == 3:
            ring(R_SINV, 1)
        if block == 4:
            @pl.when(p > 0)
            def _():
                wait(gi.at[0, 0], rsem.at[X_UP])

            @pl.when(p < 3)
            def _():
                wait(gi.at[0, 0], rsem.at[X_DOWN])

            for k in Z_ORDER:
                send(gi.at[z, pl.ds(1, 2)], gi.at[z, pl.ds(1, 2)], X_IDX2, z_peer(k)[1])
    tst[1] = w[pl.ds(CELLS - FACE, FACE)]

    def combine(value):
        return jnp.concatenate(
            [value[:32, :FACE] - value[32:, FACE:], value[32:, :FACE] + value[:32, FACE:]], axis=0
        )

    load_bs.wait()
    place = pl.ds(pl.multiple_of(lax.rem(z, 4) * 32 + c * 16, 16), 16)
    for part in range(2):
        bst[part, place] = bs[part]
    given = jnp.concatenate([jnp.transpose(bst[0]), jnp.transpose(bst[1])], axis=0)
    face_first, face_last = combine(faces[0]), combine(faces[1])

    def put(item, value):
        for other in range(8):
            stage[other, item] = jnp.concatenate(
                [value[4 * other : 4 * other + 4], value[32 + 4 * other : 36 + 4 * other]], axis=0
            )

    put(0, combine(towards))
    put(1, given)
    for k in Z_ORDER:
        other, device = z_peer(k)
        send(stage.at[other, pl.ds(0, 2)], kb.at[z, pl.ds(0, 2)], X_BASE, device)

    @pl.when(p == 2)
    def _():
        send(tst.at[1], gm.at[S_T, z], X_T, (3, front))

    @pl.when(p < 2)
    def _():
        send(tst.at[1], gm.at[S_T2, z], X_T2, (p + 1, front))

    ring(R_SINV, 2)
    wait(gm.at[S_T, 0], rsem.at[X_T])

    @pl.when(p > 0)
    def _():
        ring(S_T, 0)

    ahead_t = gm[S_T, z]
    put(2, jnp.where(p < 3, face_last, face_first))
    put(3, jnp.where(p == 0, combine(dot(face_last.astype(BF16), ahead_t)), face_first))
    for k in Z_ORDER:
        other, device = z_peer(k)
        send(stage.at[other, pl.ds(2, 2)], kb.at[z, pl.ds(2, 2)], X_BASE2, device)
    kb[z] = stage[z]
    outs = []
    for side, start in enumerate(starts):
        total = jnp.zeros((2 * FACE, 2 * FACE), F32)
        for block in range(5):
            rows, cols = pl.ds(block * BLOCK, BLOCK), pl.ds(start, FACE)
            both = jnp.concatenate([inv[0, rows, cols], inv[1, rows, cols]], axis=1)
            total = total + lax.dot_general(
                link[block * BLOCK : (block + 1) * BLOCK], both, TN, preferred_element_type=F32
            )
        outs.append(
            jnp.concatenate(
                [total[:FACE, :FACE] - total[FACE:, FACE:], total[:FACE, FACE:] + total[FACE:, :FACE]], axis=1
            )
        )
    gm[S_O, z] = jnp.where(p < 3, outs[1], outs[0]).astype(BF16)
    gm[S_O2, z] = outs[0].astype(BF16)
    low, high = pl.ds(0, FACE), pl.ds(CELLS - FACE, FACE)
    d_ff = jnp.concatenate([inv[0, low, low], inv[1, low, low]], axis=1)
    gm[S_DFF, z] = d_ff
    gm[S_D2, z] = jnp.concatenate([inv[0, high, low], inv[1, high, low]], axis=1)
    gm[S_D, z] = jnp.where(p < 3, jnp.concatenate([inv[0, low, high], inv[1, low, high]], axis=1), d_ff)
    ring(R_SINV, 3)

    @pl.when(p == 0)
    def _():
        tall = jnp.concatenate([outs[1][:, :FACE], outs[1][:, FACE:]], axis=0).astype(BF16)
        both = dot(tall, ahead_t)
        gm[S_T, z] = jnp.concatenate(
            [both[:FACE, :FACE] - both[FACE:, FACE:], both[FACE:, :FACE] + both[:FACE, FACE:]], axis=1
        ).astype(BF16)
        ring(S_T, 0)

    ring(S_O, 0)

    @pl.when(p > 0)
    def _():
        ring(S_D, 0)

    unknown = lax.broadcasted_iota(jnp.int32, (SEP, FACE), 0)

    def select(dst, item, by_row=False):
        for leaf in range(8):
            row = gi[leaf, item]
            if by_row:
                row = ((row >> 8) * 2 + ((row >> 4) & 1)) * 128 + ((row >> 5) & 7) * 16 + (row & 15)
            dst[:, leaf * FACE : (leaf + 1) * FACE] = jnp.where(unknown == row, 1.0, 0.0).astype(BF16)

    wait(gi.at[pl.ds(0, 7), 0], rsem.at[X_IDX])
    select(ptb, 0)

    sign = jnp.where(lax.broadcasted_iota(jnp.int32, (8, SEP), 0) < 4, -1.0, 1.0)

    def leafwise(vector, slot):
        parts = [dot(vector[:, leaf * FACE : (leaf + 1) * FACE], gm[slot, leaf]) for leaf in range(8)]
        direct = jnp.concatenate([v[:, :FACE] for v in parts], axis=1)
        crossed = jnp.concatenate([v[:, FACE:] for v in parts], axis=1)
        return direct + sign * jnp.roll(crossed, 4, axis=0)

    def fold(value):
        half = value.shape[1] // 2
        return jnp.concatenate([value[:, :half], value[:, half:]], axis=0).astype(BF16)

    def unfold(value):
        value = value.astype(F32)
        return jnp.concatenate([value[:8], value[8:]], axis=1)

    def scatter(value, matrix):
        return lax.dot_general(value.astype(BF16), matrix[...], NT, preferred_element_type=F32)

    def gather(value):
        return dot(value.astype(BF16), pto[...])

    def solve(turn, arrived, before, meanwhile):
        before()
        wait(pbuf.at[turn, pl.ds(0, arrived)], rsem.at[X_PART + turn])
        total = pbuf[turn, 0].astype(F32)
        for other in range(1, 8):
            total = total + pbuf[turn, other].astype(F32)
        reduced = unfold(total).astype(BF16)
        both = lax.dot_general(reduced, gs[...].reshape(2 * FACE, SEP), NT, preferred_element_type=F32)
        mine = both[:, :FACE] + sign[:, :FACE] * jnp.roll(both[:, FACE:], 4, axis=0)
        sbuf[turn, g] = mine
        for k in G_ORDER[:7]:
            send(sbuf.at[turn, g], sbuf.at[turn, g], X_SOL + turn, g_peer(k, p))
        meanwhile()
        wait(sbuf.at[turn, pl.ds(0, 7)], rsem.at[X_SOL + turn])
        return jnp.concatenate([sbuf[turn, other] for other in range(8)], axis=1)

    def onward(face, matrix, slot, which, turn, panel):
        face_low = face.astype(BF16)
        pout[which] = fold(-scatter(leafwise(face_low, slot), matrix))
        for k in G_ORDER:
            send(pout.at[which], pbuf.at[turn, g], X_PART + turn, g_peer(k, panel))
        yout[which] = fold(face)
        send(yout.at[which], yin.at[turn], X_Y + turn, (panel, front))

    def faces_back():
        for item in range(2):
            face = unfold(yin[item + 1])
            for leaf in range(8):
                hstage[leaf, item] = face[:, leaf * FACE : (leaf + 1) * FACE]
        for k in Z_ORDER:
            other, device = z_peer(k)
            send(hstage.at[other], hk.at[z], X_FACES, device)
        hk[z] = hstage[z]

    first_set(1)
    wait(kb.at[pl.ds(0, 7), pl.ds(0, 2)], rsem.at[X_BASE])
    own = -scatter(jnp.concatenate([kb[leaf, 0] for leaf in range(8)], axis=1), ptb)
    given_low = (kb[0, 1] + kb[1, 1]) + (kb[2, 1] + kb[3, 1])
    given_high = (kb[4, 1] + kb[5, 1]) + (kb[6, 1] + kb[7, 1])
    own = own + jnp.concatenate(
        [jnp.where(x == other // 2, given_low if other % 2 == 0 else given_high, 0.0) for other in range(8)], axis=1
    )
    pbuf[0, g] = fold(own)
    for k in G_ORDER[:7]:
        send(pbuf.at[0, g], pbuf.at[0, g], X_PART, g_peer(k, p))

    @pl.when(p == 0)
    def _():
        yin[1] = jnp.zeros((16, SEP // 2), BF16)

    @pl.when(p == 3)
    def _():
        yin[2] = jnp.zeros((16, SEP // 2), BF16)

    def base_before():
        select(pto, 0, by_row=True)
        ring_end(R_SINV)
        first_set(2)

    def base_meanwhile():
        wait(gi.at[pl.ds(0, 7), pl.ds(1, 2)], rsem.at[X_IDX2])

        @pl.when(p < 3)
        def _():
            select(pta, 1)

        @pl.when(p == 3)
        def _():
            select(pta, 2)

        first_set(3)
        wait(kb.at[pl.ds(0, 7), pl.ds(2, 2)], rsem.at[X_BASE2])
        acca[...] = jnp.concatenate([kb[leaf, 2] for leaf in range(8)], axis=1)
        accb[...] = jnp.concatenate([kb[leaf, 3] for leaf in range(8)], axis=1)

    stot[...] = solve(0, 7, base_before, base_meanwhile)

    @pl.when(middle)
    def _():
        wait(gm.at[S_T2, 0], rsem.at[X_T2])
        second_set(0)
        second_set(1)

    @pl.when(p > 0)
    def _():
        def meanwhile():
            wait(yin.at[1], rsem.at[X_Y + 1])
            ring_end(S_D)
            acca[...] += leafwise(unfold(yin[1]).astype(BF16), S_D)

        stot[...] += solve(1, 8, lambda: None, meanwhile)

    @pl.when(p == 0)
    def _():
        pick = gather(stot[...]).astype(BF16)
        ring_end(S_T)
        pout[0] = fold(scatter(leafwise(pick, S_T) - accb[...], pta))
        for k in G_ORDER:
            send(pout.at[0], pbuf.at[1, g], X_PART + 1, g_peer(k, 1))
        ring_end(S_O)
        yout[0] = fold(acca[...] - leafwise(pick, S_O))
        send(yout.at[0], yin.at[1], X_Y + 1, (1, front))

    @pl.when(p > 0)
    def _():
        ring_end(S_O)
        ring_end(S_T)
        onward(acca[...] - leafwise(gather(stot[...]).astype(BF16), S_O), pta, S_T, 0, turn_ahead, ahead)

    @pl.when(middle)
    def _():
        select(ptz, 2)
        second_set(2)
        second_set(3)
        for slot in SECOND_SET:
            ring_end(slot)
        accb[...] += leafwise(unfold(yin[1]).astype(BF16), S_DFF)

    @pl.when(p < 3)
    def _():
        def meanwhile():
            wait(yin.at[2], rsem.at[X_Y + 2])
            faces_back()

            @pl.when(p > 0)
            def _():
                accb[...] += leafwise(unfold(yin[2]).astype(BF16), S_D2)

        stot[...] += solve(2, 8, lambda: None, meanwhile)

    @pl.when(p == 3)
    def _():
        faces_back()

    picked = gather(stot[...])

    @pl.when(middle)
    def _():
        onward(accb[...] - leafwise(picked.astype(BF16), S_O2), ptz, S_T2, 1, 2, p - 1)

    own_sep = sbuf[0, g]
    own_sep = own_sep + jnp.where(p > 0, sbuf[1, g], 0.0)
    own_sep = own_sep + jnp.where(p < 3, sbuf[2, g], 0.0)
    for leaf in range(8):
        cols = slice(leaf * FACE, (leaf + 1) * FACE)
        fstage[leaf, 0] = picked[:, cols]
        fstage[leaf, 1] = own_sep
    for k in Z_ORDER:
        other, device = z_peer(k)
        send(fstage.at[other], fk.at[z], X_FINAL, device)
    fk[z] = fstage[z]

    def rows_of(ref, item):
        tops = [ref[other, item][:4] for other in range(8)]
        bottoms = [ref[other, item][4:] for other in range(8)]
        return jnp.concatenate(tops, axis=0), jnp.concatenate(bottoms, axis=0)

    wait(hk.at[pl.ds(0, 7)], rsem.at[X_FACES])
    add_low = jnp.concatenate(rows_of(hk, 0), axis=0)
    add_high = jnp.concatenate(rows_of(hk, 1), axis=0)
    wait(fk.at[pl.ds(0, 7)], rsem.at[X_FINAL])
    pick_re, pick_im = rows_of(fk, 0)
    doubled = jnp.concatenate(
        [jnp.concatenate([pick_re, -pick_im], axis=1), jnp.concatenate([pick_im, pick_re], axis=1)], axis=0
    ).astype(BF16)
    side = rhs[...].reshape(64, CELLS) - lax.dot_general(doubled, link, NT, preferred_element_type=F32)
    side = jnp.concatenate(
        [side[:, :FACE] + add_low, side[:, FACE : CELLS - FACE], side[:, CELLS - FACE :] + add_high], axis=1
    ).astype(BF16)
    for block in range(5):
        cols = pl.ds(block * BLOCK, BLOCK)
        real = dot(side, inv[0, :, cols])
        imag = dot(side, inv[1, :, cols])
        out_ref[0, :, cols] = real[:32] - imag[32:]
        out_ref[1, :, cols] = real[32:] + imag[:32]

    for part, value in enumerate(rows_of(fk, 1)):
        bst[part] = jnp.transpose(value)
        sep_ref[part] = bst[part, pl.ds(pl.multiple_of(z * 16, 16), 16)]

    ring_left(R_SINV)
    ring_left(S_O)
    ring_left(S_T)
    wait(gi.at[pl.ds(0, 7), 0], ssem.at[X_IDX])
    wait(gi.at[pl.ds(0, 7), pl.ds(1, 2)], ssem.at[X_IDX2])
    wait(kb.at[pl.ds(0, 7), pl.ds(0, 2)], ssem.at[X_BASE])
    wait(kb.at[pl.ds(0, 7), pl.ds(0, 2)], ssem.at[X_BASE2])
    wait(hk.at[pl.ds(0, 7)], ssem.at[X_FACES])
    wait(fk.at[pl.ds(0, 7)], ssem.at[X_FINAL])
    wait(pbuf.at[0, pl.ds(0, 7)], ssem.at[X_PART])
    wait(sbuf.at[0, pl.ds(0, 7)], ssem.at[X_SOL])

    @pl.when(p > 0)
    def _():
        ring_left(S_D)
        wait(gi.at[0, 0], ssem.at[X_DOWN])
        wait(pbuf.at[2], ssem.at[X_PART + 2])
        wait(sbuf.at[1, pl.ds(0, 7)], ssem.at[X_SOL + 1])
        wait(yin.at[2], ssem.at[X_Y + 2])

    @pl.when(p < 3)
    def _():
        wait(gi.at[0, 0], ssem.at[X_UP])
        wait(pbuf.at[1], ssem.at[X_PART + 1])
        wait(sbuf.at[2, pl.ds(0, 7)], ssem.at[X_SOL + 2])
        wait(yin.at[1], ssem.at[X_Y + 1])

    @pl.when((p == 1) | (p == 3))
    def _():
        wait(tst.at[0], ssem.at[X_T])

    @pl.when(p == 2)
    def _():
        wait(tst, ssem.at[X_T])

    @pl.when(p < 2)
    def _():
        wait(tst.at[1], ssem.at[X_T2])

    @pl.when(middle)
    def _():
        for slot in SECOND_SET:
            ring_left(slot)


def local(leaf_rhs, sep_rhs, leaf_inverse, coupling, sep_index, sep_inverse):
    vmem = pl.BlockSpec(memory_space=pltpu.VMEM)
    hbm = pl.BlockSpec(memory_space=pl.ANY)
    leaf, sep = pl.pallas_call(
        kernel,
        out_shape=(jax.ShapeDtypeStruct((2, 32, CELLS), F32), jax.ShapeDtypeStruct((2, 16, 32), F32)),
        in_specs=[hbm] * 6,
        out_specs=(vmem, vmem),
        scratch_shapes=[
            pltpu.VMEM((2, 32, CELLS), F32),
            pltpu.VMEM((2, 16, 32), F32),
            pltpu.VMEM((2, CELLS, CELLS), BF16),
            pltpu.VMEM((2, CELLS, FACE), BF16),
            pltpu.VMEM((1, FACE), jnp.int32),
            pltpu.VMEM((CELLS, 2 * FACE), BF16),
            pltpu.VMEM((2, FACE, 2 * FACE), BF16),
            pltpu.VMEM((7, 8, FACE, 2 * FACE), BF16),
            pltpu.VMEM((2, 8, 16, SEP), BF16),
            pltpu.VMEM((8, 3, 1, FACE), jnp.int32),
            pltpu.VMEM((SEP, SEP), BF16),
            pltpu.VMEM((SEP, SEP), BF16),
            pltpu.VMEM((SEP, SEP), BF16),
            pltpu.VMEM((SEP, SEP), BF16),
            pltpu.VMEM((8, 4, 8, FACE), F32),
            pltpu.VMEM((8, 4, 8, FACE), F32),
            pltpu.VMEM((3, 8, 16, SEP // 2), BF16),
            pltpu.VMEM((2, 16, SEP // 2), BF16),
            pltpu.VMEM((3, 8, 8, FACE), F32),
            pltpu.VMEM((2, 16, SEP // 2), BF16),
            pltpu.VMEM((3, 16, SEP // 2), BF16),
            pltpu.VMEM((2, FACE, 32), F32),
            pltpu.VMEM((8, 2, 8, FACE), F32),
            pltpu.VMEM((8, 2, 8, FACE), F32),
            pltpu.VMEM((8, 2, 8, FACE), F32),
            pltpu.VMEM((8, 2, 8, FACE), F32),
            pltpu.VMEM((8, SEP), F32),
            pltpu.VMEM((8, SEP), F32),
            pltpu.VMEM((8, SEP), F32),
            pltpu.SemaphoreType.DMA((10,)),
            pltpu.SemaphoreType.DMA((X_COUNT,)),
            pltpu.SemaphoreType.DMA((X_COUNT,)),
            pltpu.SemaphoreType.DMA((8, 2, 4)),
            pltpu.SemaphoreType.DMA((8, 2, 4)),
        ],
        compiler_params=pltpu.CompilerParams(
            collective_id=0, has_side_effects=True, vmem_limit_bytes=56 * 2**20
        ),
    )(
        leaf_rhs[0, 0], sep_rhs[0].transpose(0, 2, 1), leaf_inverse[0, 0], coupling[0, 0], sep_index[0],
        sep_inverse[0].transpose(0, 2, 1)
    )
    return leaf[None, None], sep.transpose(0, 2, 1)[None]


def solution(mesh):
    in_specs = (
        P("panel", "front", None, None, None),
        P("panel", None, None, "front"),
        P("panel", "front", None, None, None),
        P("panel", "front", None, None, None),
        P("panel", "front", None),
        P("panel", None, None, "front"),
    )
    out_specs = (P("panel", "front", None, None, None), P("panel", None, None, "front"))
    return jax.shard_map(local, mesh=mesh, in_specs=in_specs, out_specs=out_specs, check_vma=False)
```

```python
import jax
import jax.numpy as jnp
from jax import lax
from jax.experimental import pallas as pl
from jax.experimental.pallas import tpu as pltpu
from jax.sharding import PartitionSpec as P

MESH = pl.DeviceIdType.MESH
F32 = jnp.float32
BF16 = jnp.bfloat16
FACE = 128
CELLS = 1280
SEP = 1024
BLOCK = 256
NT = (((1,), (1,)), ((), ()))
TN = (((0,), (0,)), ((), ()))

S_T, S_O, S_D, S_O2, S_T2, S_D2, S_DFF, R_SINV = range(8)
Z_ORDER, G_ORDER = (4, 3, 5, 2, 6, 1, 7), (4, 5, 2, 6, 3, 7, 1, 0)
FIRST_SET, SECOND_SET = (S_O, S_T, S_D), (S_O2, S_T2, S_D2, S_DFF)
X_UP, X_DOWN, X_IDX, X_BASE, X_T, X_T2, X_PART, X_SOL, X_Y, X_FACES, X_FINAL, X_IDX2, X_BASE2, X_COUNT = 0, 1, 2, 3, 4, 5, 6, 9, 12, 15, 16, 17, 18, 19


def dot(a, b):
    return jnp.dot(a, b, preferred_element_type=F32)


def kernel(rhs_hbm, bs_hbm, inv_hbm, cc_hbm, idx_hbm, sinv_hbm, out_ref, sep_ref,
           rhs, bs, inv, cc, idx, w, tst, gm, gs, gi, pto, ptb, pta, ptz, stage, kb, pbuf, pout, sbuf, yout, yin,
           bst, hstage, hk, fstage, fk, acca, accb, acct, stot, got, whole, lsem, ssem, rsem, rs, rr):
    p = lax.axis_index("panel")
    front = lax.axis_index("front")
    x, z, c = front // 16, lax.rem(front // 2, 8), lax.rem(front, 2)
    g = x * 2 + c
    middle = (p > 0) & (p < 3)
    ahead = jnp.where(p < 3, p + 1, 2)
    turn_ahead = jnp.where(p < 3, 1, 2)

    def z_peer(k):
        other = lax.rem(z + k, 8)
        return other, (p, (x * 8 + other) * 2 + c)

    def g_peer(k, panel):
        return panel, (lax.rem(x + k // 2, 4) * 8 + z) * 2 + lax.rem(c + k % 2, 2)

    def load(src, dst, number):
        copy = pltpu.make_async_copy(src, dst, lsem.at[number])
        copy.start()
        return copy

    load_sinv = load(sinv_hbm, gs.at[:, z], 0)
    load_idx = load(idx_hbm, idx, 1)
    load_cc = load(cc_hbm, cc, 2)
    load_inv = []
    for block in range(5):
        rows = pl.ds(block * BLOCK, BLOCK)
        load_inv.append(load(inv_hbm.at[:, rows], inv.at[:, rows], 3 + block))
        if block == 0:
            load_rhs = load(rhs_hbm, rhs, 8)
    load_bs = load(bs_hbm, bs, 9)

    barrier = pltpu.get_barrier_semaphore()

    def greet(device):
        pl.semaphore_signal(barrier, inc=1, device_id=device, device_id_type=MESH)

    for k in range(1, 8):
        greet(z_peer(k)[1])
        greet(g_peer(k, p))

    @pl.when(p > 0)
    def _():
        for k in range(8):
            greet(g_peer(k, p - 1))

    @pl.when(p < 3)
    def _():
        for k in range(8):
            greet(g_peer(k, p + 1))

    bst[...] = jnp.zeros((2, FACE, 32), F32)

    def send(src, dst, which, device):
        pltpu.make_async_remote_copy(
            src_ref=src, dst_ref=dst, send_sem=ssem.at[which], recv_sem=rsem.at[which], device_id=device, device_id_type=MESH
        ).start()

    def wait(ref, sem):
        pltpu.make_async_copy(ref, ref, sem).wait()

    onto = jnp.where(c == 0, 1, 7)

    def block_of(slot, owner):
        return gs.at[:, owner] if slot == R_SINV else gm.at[slot, owner]

    def ring(slot, step):
        for way, steps in ((0, 4), (1, 3)):
            if step < steps:
                if step > 0:
                    wait(block_of(slot, 0), rr.at[slot, way, step - 1])
                owner = lax.rem(z + step * (8 - onto if way == 0 else onto), 8)
                pltpu.make_async_remote_copy(
                    src_ref=block_of(slot, owner), dst_ref=block_of(slot, owner), send_sem=rs.at[slot, way, step],
                    recv_sem=rr.at[slot, way, step], device_id=z_peer(onto if way == 0 else 8 - onto)[1], device_id_type=MESH
                ).start()

    def ring_end(slot):
        wait(block_of(slot, 0), rr.at[slot, 0, 3])
        wait(block_of(slot, 0), rr.at[slot, 1, 2])

    def ring_left(slot):
        for way, steps in ((0, 4), (1, 3)):
            for step in range(steps):
                wait(block_of(slot, 0), rs.at[slot, way, step])

    def first_set(step):
        ring(S_T, step)

        @pl.when(p > 0)
        def _():
            ring(S_D, step)

        ring(S_O, step)

    def second_set(step):
        for slot in SECOND_SET:
            ring(slot, step)

    def begin():
        pl.semaphore_wait(barrier, 14 + jnp.where(p > 0, 8, 0) + jnp.where(p < 3, 8, 0))
        load_sinv.wait()
        ring(R_SINV, 0)
        load_idx.wait()
        own_index = idx[...]
        gi[z, 0] = own_index
        for k in Z_ORDER:
            send(gi.at[z, 0], gi.at[z, 0], X_IDX, z_peer(k)[1])

        @pl.when(p == 0)
        def _():
            gi[z, 2] = own_index

        @pl.when(p == 3)
        def _():
            gi[z, 1] = own_index

        @pl.when(p < 3)
        def _():
            send(gi.at[z, 0], gi.at[z, 2], X_UP, (p + 1, front))

        @pl.when(p > 0)
        def _():
            send(gi.at[z, 0], gi.at[z, 1], X_DOWN, (p - 1, front))

    load_cc.wait()
    load_rhs.wait()
    flat = rhs[...].reshape(64, CELLS).astype(BF16)
    towards = jnp.zeros((64, 2 * FACE), F32)
    faces = [jnp.zeros((64, 2 * FACE), F32) for _ in range(2)]
    link = jnp.concatenate([cc[0], cc[1]], axis=1)
    starts = (0, CELLS - FACE)
    for block in range(5):
        rows = pl.ds(block * BLOCK, BLOCK)
        load_inv[block].wait()
        real = dot(inv[0, rows], link)
        imag = dot(inv[1, rows], link)
        part = jnp.concatenate(
            [real[:, :FACE] - imag[:, FACE:], real[:, FACE:] + imag[:, :FACE]], axis=1
        ).astype(BF16)
        w[rows] = part
        some = flat[:, block * BLOCK : (block + 1) * BLOCK]
        towards = towards + dot(some, part)
        for side, start in enumerate(starts):
            cols = pl.ds(start, FACE)
            both = jnp.concatenate([inv[0, rows, cols], inv[1, rows, cols]], axis=1)
            faces[side] = faces[side] + dot(some, both)
        if block == 0:
            tst[0] = part[:FACE]
        if block == 1:
            begin()

            @pl.when(p > 0)
            def _():
                send(tst.at[0], gm.at[S_T, z], X_T, (p - 1, front))
        if block == 3:
            ring(R_SINV, 1)
        if block == 4:
            @pl.when(p > 0)
            def _():
                wait(gi.at[0, 0], rsem.at[X_UP])

            @pl.when(p < 3)
            def _():
                wait(gi.at[0, 0], rsem.at[X_DOWN])

            for k in Z_ORDER:
                send(gi.at[z, pl.ds(1, 2)], gi.at[z, pl.ds(1, 2)], X_IDX2, z_peer(k)[1])
    tst[1] = w[pl.ds(CELLS - FACE, FACE)]

    def combine(value):
        return jnp.concatenate(
            [value[:32, :FACE] - value[32:, FACE:], value[32:, :FACE] + value[:32, FACE:]], axis=0
        )

    load_bs.wait()
    place = pl.ds(pl.multiple_of(lax.rem(z, 4) * 32 + c * 16, 16), 16)
    for part in range(2):
        bst[part, place] = bs[part]
    given = jnp.concatenate([jnp.transpose(bst[0]), jnp.transpose(bst[1])], axis=0)
    face_first, face_last = combine(faces[0]), combine(faces[1])

    def put(item, value):
        for other in range(8):
            stage[other, item] = jnp.concatenate(
                [value[4 * other : 4 * other + 4], value[32 + 4 * other : 36 + 4 * other]], axis=0
            )

    put(0, combine(towards))
    put(1, given)
    for k in Z_ORDER:
        other, device = z_peer(k)
        send(stage.at[other, pl.ds(0, 2)], kb.at[z, pl.ds(0, 2)], X_BASE, device)

    @pl.when(p == 2)
    def _():
        send(tst.at[1], gm.at[S_T, z], X_T, (3, front))

    @pl.when(p < 2)
    def _():
        send(tst.at[1], gm.at[S_T2, z], X_T2, (p + 1, front))

    ring(R_SINV, 2)
    wait(gm.at[S_T, 0], rsem.at[X_T])

    @pl.when(p > 0)
    def _():
        ring(S_T, 0)

    ahead_t = gm[S_T, z]
    put(2, jnp.where(p < 3, face_last, face_first))
    put(3, jnp.where(p == 0, combine(dot(face_last.astype(BF16), ahead_t)), face_first))
    for k in Z_ORDER:
        other, device = z_peer(k)
        send(stage.at[other, pl.ds(2, 2)], kb.at[z, pl.ds(2, 2)], X_BASE2, device)
    kb[z] = stage[z]
    outs = []
    for side, start in enumerate(starts):
        total = jnp.zeros((2 * FACE, 2 * FACE), F32)
        for block in range(5):
            rows, cols = pl.ds(block * BLOCK, BLOCK), pl.ds(start, FACE)
            both = jnp.concatenate([inv[0, rows, cols], inv[1, rows, cols]], axis=1)
            total = total + lax.dot_general(
                link[block * BLOCK : (block + 1) * BLOCK], both, TN, preferred_element_type=F32
            )
        outs.append(
            jnp.concatenate(
                [total[:FACE, :FACE] - total[FACE:, FACE:], total[:FACE, FACE:] + total[FACE:, :FACE]], axis=1
            )
        )
    gm[S_O, z] = jnp.where(p < 3, outs[1], outs[0]).astype(BF16)
    gm[S_O2, z] = outs[0].astype(BF16)
    low, high = pl.ds(0, FACE), pl.ds(CELLS - FACE, FACE)
    d_ff = jnp.concatenate([inv[0, low, low], inv[1, low, low]], axis=1)
    gm[S_DFF, z] = d_ff
    gm[S_D2, z] = jnp.concatenate([inv[0, high, low], inv[1, high, low]], axis=1)
    gm[S_D, z] = jnp.where(p < 3, jnp.concatenate([inv[0, low, high], inv[1, low, high]], axis=1), d_ff)
    ring(R_SINV, 3)

    @pl.when(p == 0)
    def _():
        tall = jnp.concatenate([outs[1][:, :FACE], outs[1][:, FACE:]], axis=0).astype(BF16)
        both = dot(tall, ahead_t)
        gm[S_T, z] = jnp.concatenate(
            [both[:FACE, :FACE] - both[FACE:, FACE:], both[FACE:, :FACE] + both[:FACE, FACE:]], axis=1
        ).astype(BF16)
        ring(S_T, 0)

    @pl.when(p > 0)
    def _():
        ring(S_D, 0)

    ring(S_O, 0)

    unknown = lax.broadcasted_iota(jnp.int32, (SEP, FACE), 0)

    def select(dst, item, by_row=False):
        for leaf in range(8):
            row = gi[leaf, item]
            if by_row:
                row = ((row >> 8) * 2 + ((row >> 4) & 1)) * 128 + ((row >> 5) & 7) * 16 + (row & 15)
            dst[:, leaf * FACE : (leaf + 1) * FACE] = jnp.where(unknown == row, 1.0, 0.0).astype(BF16)

    wait(gi.at[pl.ds(0, 7), 0], rsem.at[X_IDX])
    select(ptb, 0)

    sign = jnp.where(lax.broadcasted_iota(jnp.int32, (8, SEP), 0) < 4, -1.0, 1.0)

    def leafwise(vector, slot):
        parts = [dot(vector[:, leaf * FACE : (leaf + 1) * FACE], got[leaf] if slot is None else gm[slot, leaf]) for leaf in range(8)]
        direct = jnp.concatenate([v[:, :FACE] for v in parts], axis=1)
        crossed = jnp.concatenate([v[:, FACE:] for v in parts], axis=1)
        return direct + sign * jnp.roll(crossed, 4, axis=0)

    def fold(value):
        half = value.shape[1] // 2
        return jnp.concatenate([value[:, :half], value[:, half:]], axis=0).astype(BF16)

    def unfold(value):
        value = value.astype(F32)
        return jnp.concatenate([value[:8], value[8:]], axis=1)

    def scatter(value, matrix):
        return lax.dot_general(value.astype(BF16), matrix[...], NT, preferred_element_type=F32)

    def gather(value):
        return dot(value.astype(BF16), pto[...])

    def solve(turn, arrived, before, meanwhile):
        before()
        wait(pbuf.at[turn, pl.ds(0, arrived)], rsem.at[X_PART + turn])
        total = pbuf[turn, 0].astype(F32)
        for other in range(1, 8):
            total = total + pbuf[turn, other].astype(F32)
        reduced = unfold(total).astype(BF16)
        both = lax.dot_general(reduced, gs[...].reshape(2 * FACE, SEP), NT, preferred_element_type=F32)
        mine = both[:, :FACE] + sign[:, :FACE] * jnp.roll(both[:, FACE:], 4, axis=0)
        sbuf[turn, g] = mine
        for k in G_ORDER[:7]:
            send(sbuf.at[turn, g], sbuf.at[turn, g], X_SOL + turn, g_peer(k, p))
        meanwhile()
        wait(sbuf.at[turn, pl.ds(0, 7)], rsem.at[X_SOL + turn])
        return jnp.concatenate([sbuf[turn, other] for other in range(8)], axis=1)

    def onward(face, matrix, slot, which, turn, panel):
        face_low = face.astype(BF16)
        pout[which] = fold(-scatter(leafwise(face_low, slot), matrix))
        for k in G_ORDER:
            send(pout.at[which], pbuf.at[turn, g], X_PART + turn, g_peer(k, panel))
        yout[which] = fold(face)
        send(yout.at[which], yin.at[turn], X_Y + turn, (panel, front))

    def faces_back():
        for item in range(2):
            face = unfold(yin[item + 1])
            for leaf in range(8):
                hstage[leaf, item] = face[:, leaf * FACE : (leaf + 1) * FACE]
        for k in Z_ORDER:
            other, device = z_peer(k)
            send(hstage.at[other], hk.at[z], X_FACES, device)
        hk[z] = hstage[z]

    def through(o_slot, t_slot):
        for leaf in range(8):
            out = gm[o_slot, leaf]
            both = dot(jnp.concatenate([out[:, :FACE], out[:, FACE:]], axis=0), gm[t_slot, leaf])
            got[leaf] = jnp.concatenate(
                [both[:FACE, :FACE] - both[FACE:, FACE:], both[FACE:, :FACE] + both[:FACE, FACE:]], axis=1
            ).astype(BF16)

    def onward_folded(pick, acc, matrix, o_slot, which, turn, panel):
        pout[which] = fold(scatter(leafwise(pick, None) - acct[...], matrix))
        for k in G_ORDER:
            send(pout.at[which], pbuf.at[turn, g], X_PART + turn, g_peer(k, panel))
        yout[which] = fold(acc[...] - leafwise(pick, o_slot))
        send(yout.at[which], yin.at[turn], X_Y + turn, (panel, front))

    first_set(1)
    wait(kb.at[pl.ds(0, 7), pl.ds(0, 2)], rsem.at[X_BASE])
    own = -scatter(jnp.concatenate([kb[leaf, 0] for leaf in range(8)], axis=1), ptb)
    given_low = (kb[0, 1] + kb[1, 1]) + (kb[2, 1] + kb[3, 1])
    given_high = (kb[4, 1] + kb[5, 1]) + (kb[6, 1] + kb[7, 1])
    own = own + jnp.concatenate(
        [jnp.where(x == other // 2, given_low if other % 2 == 0 else given_high, 0.0) for other in range(8)], axis=1
    )
    pbuf[0, g] = fold(own)
    for k in G_ORDER[:7]:
        send(pbuf.at[0, g], pbuf.at[0, g], X_PART, g_peer(k, p))

    @pl.when(p == 0)
    def _():
        yin[1] = jnp.zeros((16, SEP // 2), BF16)

    @pl.when(p == 3)
    def _():
        yin[2] = jnp.zeros((16, SEP // 2), BF16)

    def base_before():
        select(pto, 0, by_row=True)
        ring_end(R_SINV)
        first_set(2)

    def base_meanwhile():
        wait(gi.at[pl.ds(0, 7), pl.ds(1, 2)], rsem.at[X_IDX2])

        @pl.when(p < 3)
        def _():
            select(pta, 1)

        @pl.when(p == 3)
        def _():
            select(pta, 2)

        first_set(3)
        wait(kb.at[pl.ds(0, 7), pl.ds(2, 2)], rsem.at[X_BASE2])
        acca[...] = jnp.concatenate([kb[leaf, 2] for leaf in range(8)], axis=1)
        accb[...] = jnp.concatenate([kb[leaf, 3] for leaf in range(8)], axis=1)

    stot[...] = solve(0, 7, base_before, base_meanwhile)

    @pl.when(p == 2)
    def _():
        wait(gm.at[S_T2, 0], rsem.at[X_T2])
        second_set(0)
        second_set(1)

    @pl.when(p > 0)
    def _():
        def meanwhile():
            wait(yin.at[1], rsem.at[X_Y + 1])
            ring_end(S_D)
            acca[...] += leafwise(unfold(yin[1]).astype(BF16), S_D)

            @pl.when(p > 1)
            def _():
                acct[...] = leafwise(acca[...].astype(BF16), S_T)

        @pl.when(p > 1)
        def _():
            ring_end(S_O)
            ring_end(S_T)
            through(S_O, S_T)

        stot[...] += solve(1, 8, lambda: None, meanwhile)

    @pl.when(p == 0)
    def _():
        pick = gather(stot[...]).astype(BF16)
        ring_end(S_T)
        pout[0] = fold(scatter(leafwise(pick, S_T) - accb[...], pta))
        for k in G_ORDER:
            send(pout.at[0], pbuf.at[1, g], X_PART + 1, g_peer(k, 1))
        ring_end(S_O)
        yout[0] = fold(acca[...] - leafwise(pick, S_O))
        send(yout.at[0], yin.at[1], X_Y + 1, (1, front))
        sides = rhs[...].reshape(64, CELLS).astype(BF16)
        links = jnp.concatenate([cc[0], cc[1]], axis=1)
        for block in range(5):
            cols = pl.ds(block * BLOCK, BLOCK)
            real = dot(sides, inv[0, :, cols])
            imag = dot(sides, inv[1, :, cols])
            out_ref[0, :, cols] = real[:32] - imag[32:]
            out_ref[1, :, cols] = real[32:] + imag[:32]
            by_real = lax.dot_general(links, inv[0, :, cols], TN, preferred_element_type=F32)
            by_imag = lax.dot_general(links, inv[1, :, cols], TN, preferred_element_type=F32)
            whole[:FACE, cols] = (by_real[:FACE] - by_imag[FACE:]).astype(BF16)
            whole[FACE:, cols] = (by_imag[:FACE] + by_real[FACE:]).astype(BF16)

    @pl.when(p == 1)
    def _():
        ring_end(S_O)
        ring_end(S_T)
        onward(acca[...] - leafwise(gather(stot[...]).astype(BF16), S_O), pta, S_T, 0, 1, 2)

    @pl.when(p > 1)
    def _():
        onward_folded(gather(stot[...]).astype(BF16), acca, pta, S_O, 0, turn_ahead, ahead)

    @pl.when(p == 1)
    def _():
        wait(gm.at[S_T2, 0], rsem.at[X_T2])
        second_set(0)
        second_set(1)

    @pl.when(middle)
    def _():
        select(ptz, 2)
        second_set(2)
        second_set(3)
        for slot in SECOND_SET:
            ring_end(slot)
        accb[...] += leafwise(unfold(yin[1]).astype(BF16), S_DFF)
        through(S_O2, S_T2)

    @pl.when(p < 3)
    def _():
        def meanwhile():
            wait(yin.at[2], rsem.at[X_Y + 2])
            faces_back()

            @pl.when(p > 0)
            def _():
                accb[...] += leafwise(unfold(yin[2]).astype(BF16), S_D2)
                acct[...] = leafwise(accb[...].astype(BF16), S_T2)

        stot[...] += solve(2, 8, lambda: None, meanwhile)

    @pl.when(p == 3)
    def _():
        faces_back()

    picked = gather(stot[...])

    @pl.when(middle)
    def _():
        onward_folded(picked.astype(BF16), accb, ptz, S_O2, 1, 2, p - 1)

    own_sep = sbuf[0, g]
    own_sep = own_sep + jnp.where(p > 0, sbuf[1, g], 0.0)
    own_sep = own_sep + jnp.where(p < 3, sbuf[2, g], 0.0)
    for leaf in range(8):
        cols = slice(leaf * FACE, (leaf + 1) * FACE)
        fstage[leaf, 0] = picked[:, cols]
        fstage[leaf, 1] = own_sep
    for k in Z_ORDER:
        other, device = z_peer(k)
        send(fstage.at[other], fk.at[z], X_FINAL, device)
    fk[z] = fstage[z]

    def rows_of(ref, item):
        tops = [ref[other, item][:4] for other in range(8)]
        bottoms = [ref[other, item][4:] for other in range(8)]
        return jnp.concatenate(tops, axis=0), jnp.concatenate(bottoms, axis=0)

    def doubled(ref, item):
        re, im = rows_of(ref, item)
        return jnp.concatenate(
            [jnp.concatenate([re, -im], axis=1), jnp.concatenate([im, re], axis=1)], axis=0
        ).astype(BF16)

    wait(hk.at[pl.ds(0, 7)], rsem.at[X_FACES])

    @pl.when(p == 0)
    def _():
        face = doubled(hk, 1)
        for block in range(5):
            cols = pl.ds(block * BLOCK, BLOCK)
            both = dot(face, jnp.concatenate([inv[0, high, cols], inv[1, high, cols]], axis=0))
            out_ref[0, :, cols] += both[:32]
            out_ref[1, :, cols] += both[32:]

    wait(fk.at[pl.ds(0, 7)], rsem.at[X_FINAL])

    @pl.when(p == 0)
    def _():
        both = dot(doubled(fk, 0), whole[...])
        out_ref[0] -= both[:32]
        out_ref[1] -= both[32:]

    @pl.when(p > 0)
    def _():
        links = jnp.concatenate([cc[0], cc[1]], axis=1)
        side = rhs[...].reshape(64, CELLS) - lax.dot_general(
            doubled(fk, 0), links, NT, preferred_element_type=F32
        )
        add_low = jnp.concatenate(rows_of(hk, 0), axis=0)
        add_high = jnp.concatenate(rows_of(hk, 1), axis=0)
        side = jnp.concatenate(
            [side[:, :FACE] + add_low, side[:, FACE : CELLS - FACE], side[:, CELLS - FACE :] + add_high], axis=1
        ).astype(BF16)
        for block in range(5):
            cols = pl.ds(block * BLOCK, BLOCK)
            real = dot(side, inv[0, :, cols])
            imag = dot(side, inv[1, :, cols])
            out_ref[0, :, cols] = real[:32] - imag[32:]
            out_ref[1, :, cols] = real[32:] + imag[:32]

    for part, value in enumerate(rows_of(fk, 1)):
        bst[part] = jnp.transpose(value)
        sep_ref[part] = bst[part, pl.ds(pl.multiple_of(z * 16, 16), 16)]

    ring_left(R_SINV)
    ring_left(S_O)
    ring_left(S_T)
    wait(gi.at[pl.ds(0, 7), 0], ssem.at[X_IDX])
    wait(gi.at[pl.ds(0, 7), pl.ds(1, 2)], ssem.at[X_IDX2])
    wait(kb.at[pl.ds(0, 7), pl.ds(0, 2)], ssem.at[X_BASE])
    wait(kb.at[pl.ds(0, 7), pl.ds(0, 2)], ssem.at[X_BASE2])
    wait(hk.at[pl.ds(0, 7)], ssem.at[X_FACES])
    wait(fk.at[pl.ds(0, 7)], ssem.at[X_FINAL])
    wait(pbuf.at[0, pl.ds(0, 7)], ssem.at[X_PART])
    wait(sbuf.at[0, pl.ds(0, 7)], ssem.at[X_SOL])

    @pl.when(p > 0)
    def _():
        ring_left(S_D)
        wait(gi.at[0, 0], ssem.at[X_DOWN])
        wait(pbuf.at[2], ssem.at[X_PART + 2])
        wait(sbuf.at[1, pl.ds(0, 7)], ssem.at[X_SOL + 1])
        wait(yin.at[2], ssem.at[X_Y + 2])

    @pl.when(p < 3)
    def _():
        wait(gi.at[0, 0], ssem.at[X_UP])
        wait(pbuf.at[1], ssem.at[X_PART + 1])
        wait(sbuf.at[2, pl.ds(0, 7)], ssem.at[X_SOL + 2])
        wait(yin.at[1], ssem.at[X_Y + 1])

    @pl.when((p == 1) | (p == 3))
    def _():
        wait(tst.at[0], ssem.at[X_T])

    @pl.when(p == 2)
    def _():
        wait(tst, ssem.at[X_T])

    @pl.when(p < 2)
    def _():
        wait(tst.at[1], ssem.at[X_T2])

    @pl.when(middle)
    def _():
        for slot in SECOND_SET:
            ring_left(slot)


def local(leaf_rhs, sep_rhs, leaf_inverse, coupling, sep_index, sep_inverse):
    vmem = pl.BlockSpec(memory_space=pltpu.VMEM)
    hbm = pl.BlockSpec(memory_space=pl.ANY)
    leaf, sep = pl.pallas_call(
        kernel,
        out_shape=(jax.ShapeDtypeStruct((2, 32, CELLS), F32), jax.ShapeDtypeStruct((2, 16, 32), F32)),
        in_specs=[hbm] * 6,
        out_specs=(vmem, vmem),
        scratch_shapes=[
            pltpu.VMEM((2, 32, CELLS), F32),
            pltpu.VMEM((2, 16, 32), F32),
            pltpu.VMEM((2, CELLS, CELLS), BF16),
            pltpu.VMEM((2, CELLS, FACE), BF16),
            pltpu.VMEM((1, FACE), jnp.int32),
            pltpu.VMEM((CELLS, 2 * FACE), BF16),
            pltpu.VMEM((2, FACE, 2 * FACE), BF16),
            pltpu.VMEM((7, 8, FACE, 2 * FACE), BF16),
            pltpu.VMEM((2, 8, 16, SEP), BF16),
            pltpu.VMEM((8, 3, 1, FACE), jnp.int32),
            pltpu.VMEM((SEP, SEP), BF16),
            pltpu.VMEM((SEP, SEP), BF16),
            pltpu.VMEM((SEP, SEP), BF16),
            pltpu.VMEM((SEP, SEP), BF16),
            pltpu.VMEM((8, 4, 8, FACE), F32),
            pltpu.VMEM((8, 4, 8, FACE), F32),
            pltpu.VMEM((3, 8, 16, SEP // 2), BF16),
            pltpu.VMEM((2, 16, SEP // 2), BF16),
            pltpu.VMEM((3, 8, 8, FACE), F32),
            pltpu.VMEM((2, 16, SEP // 2), BF16),
            pltpu.VMEM((3, 16, SEP // 2), BF16),
            pltpu.VMEM((2, FACE, 32), F32),
            pltpu.VMEM((8, 2, 8, FACE), F32),
            pltpu.VMEM((8, 2, 8, FACE), F32),
            pltpu.VMEM((8, 2, 8, FACE), F32),
            pltpu.VMEM((8, 2, 8, FACE), F32),
            pltpu.VMEM((8, SEP), F32),
            pltpu.VMEM((8, SEP), F32),
            pltpu.VMEM((8, SEP), F32),
            pltpu.VMEM((8, SEP), F32),
            pltpu.VMEM((8, FACE, 2 * FACE), BF16),
            pltpu.VMEM((2 * FACE, CELLS), BF16),
            pltpu.SemaphoreType.DMA((10,)),
            pltpu.SemaphoreType.DMA((X_COUNT,)),
            pltpu.SemaphoreType.DMA((X_COUNT,)),
            pltpu.SemaphoreType.DMA((8, 2, 4)),
            pltpu.SemaphoreType.DMA((8, 2, 4)),
        ],
        compiler_params=pltpu.CompilerParams(
            collective_id=0, has_side_effects=True, vmem_limit_bytes=56 * 2**20
        ),
    )(
        leaf_rhs[0, 0], sep_rhs[0].transpose(0, 2, 1), leaf_inverse[0, 0], coupling[0, 0], sep_index[0],
        sep_inverse[0].transpose(0, 2, 1)
    )
    return leaf[None, None], sep.transpose(0, 2, 1)[None]


def solution(mesh):
    in_specs = (
        P("panel", "front", None, None, None),
        P("panel", None, None, "front"),
        P("panel", "front", None, None, None),
        P("panel", "front", None, None, None),
        P("panel", "front", None),
        P("panel", None, None, "front"),
    )
    out_specs = (P("panel", "front", None, None, None), P("panel", None, None, "front"))
    return jax.shard_map(local, mesh=mesh, in_specs=in_specs, out_specs=out_specs, check_vma=False)
```

```python
import jax
import jax.numpy as jnp
from jax import lax
from jax.experimental import pallas as pl
from jax.experimental.pallas import tpu as pltpu
from jax.sharding import PartitionSpec as P

MESH = pl.DeviceIdType.MESH
F32 = jnp.float32
BF16 = jnp.bfloat16
FACE = 128
CELLS = 1280
SEP = 1024
BLOCK = 256
NT = (((1,), (1,)), ((), ()))
TN = (((0,), (0,)), ((), ()))

S_T, S_O, S_D, S_O2, S_T2, S_D2, S_DFF, R_SINV, R_SINV2 = range(9)
Z_ORDER, G_ORDER = (4, 3, 5, 2, 6, 1, 7), (4, 5, 2, 6, 3, 7, 1, 0)
FIRST_SET, SECOND_SET = (S_O, S_T, S_D), (S_O2, S_T2, S_D2, S_DFF)
X_UP, X_DOWN, X_IDX, X_BASE, X_T, X_T2, X_PART, X_SOL, X_Y, X_FACES, X_FINAL, X_IDX2, X_BASE2, X_COUNT = 0, 1, 2, 3, 4, 5, 6, 9, 12, 15, 16, 17, 18, 19


def dot(a, b):
    return jnp.dot(a, b, preferred_element_type=F32)


def kernel(rhs_hbm, bs_hbm, inv_hbm, cc_hbm, idx_hbm, sinv_hbm, out_ref, sep_ref,
           rhs, bs, inv, cc, idx, w, tst, gm, gs, gi, pto, ptb, pta, ptz, stage, kb, pbuf, pout, sbuf, yout, yin,
           bst, hstage, hk, fstage, fk, acca, accb, acct, stot, got, whole, lsem, ssem, rsem, rs, rr):
    p = lax.axis_index("panel")
    front = lax.axis_index("front")
    x, z, c = front // 16, lax.rem(front // 2, 8), lax.rem(front, 2)
    g = x * 2 + c
    middle = (p > 0) & (p < 3)
    ahead = jnp.where(p < 3, p + 1, 2)
    turn_ahead = jnp.where(p < 3, 1, 2)

    def z_peer(k):
        other = lax.rem(z + k, 8)
        return other, (p, (x * 8 + other) * 2 + c)

    def g_peer(k, panel):
        return panel, (lax.rem(x + k // 2, 4) * 8 + z) * 2 + lax.rem(c + k % 2, 2)

    def load(src, dst, number):
        copy = pltpu.make_async_copy(src, dst, lsem.at[number])
        copy.start()
        return copy

    load_sinv = load(sinv_hbm, gs.at[:, z], 0)
    load_idx = load(idx_hbm, idx, 1)
    load_cc = load(cc_hbm, cc, 2)
    load_inv = []
    for block in range(5):
        rows = pl.ds(block * BLOCK, BLOCK)
        load_inv.append(load(inv_hbm.at[:, rows], inv.at[:, rows], 3 + block))
        if block == 0:
            load_rhs = load(rhs_hbm, rhs, 8)
    load_bs = load(bs_hbm, bs, 9)

    barrier = pltpu.get_barrier_semaphore()

    def greet(device):
        pl.semaphore_signal(barrier, inc=1, device_id=device, device_id_type=MESH)

    for k in range(1, 8):
        greet(z_peer(k)[1])
        greet(g_peer(k, p))

    @pl.when(p > 0)
    def _():
        for k in range(8):
            greet(g_peer(k, p - 1))

    @pl.when(p < 3)
    def _():
        for k in range(8):
            greet(g_peer(k, p + 1))

    bst[...] = jnp.zeros((2, FACE, 32), F32)

    def send(src, dst, which, device):
        pltpu.make_async_remote_copy(
            src_ref=src, dst_ref=dst, send_sem=ssem.at[which], recv_sem=rsem.at[which], device_id=device, device_id_type=MESH
        ).start()

    def wait(ref, sem):
        pltpu.make_async_copy(ref, ref, sem).wait()

    onto = jnp.where(c == 0, 1, 7)

    def block_of(slot, owner):
        return gs.at[slot - R_SINV, owner] if slot >= R_SINV else gm.at[slot, owner]

    def ring(slot, step):
        for way, steps in ((0, 4), (1, 3)):
            if step < steps:
                if step > 0:
                    wait(block_of(slot, 0), rr.at[slot, way, step - 1])
                owner = lax.rem(z + step * (8 - onto if way == 0 else onto), 8)
                pltpu.make_async_remote_copy(
                    src_ref=block_of(slot, owner), dst_ref=block_of(slot, owner), send_sem=rs.at[slot, way, step],
                    recv_sem=rr.at[slot, way, step], device_id=z_peer(onto if way == 0 else 8 - onto)[1], device_id_type=MESH
                ).start()

    def ring_end(slot):
        wait(block_of(slot, 0), rr.at[slot, 0, 3])
        wait(block_of(slot, 0), rr.at[slot, 1, 2])

    def ring_left(slot):
        for way, steps in ((0, 4), (1, 3)):
            for step in range(steps):
                wait(block_of(slot, 0), rs.at[slot, way, step])

    def first_set(step):
        ring(S_T, step)

        @pl.when(p > 0)
        def _():
            ring(S_D, step)

        ring(S_O, step)

    def second_set(step):
        for slot in SECOND_SET:
            ring(slot, step)

    def begin():
        pl.semaphore_wait(barrier, 14 + jnp.where(p > 0, 8, 0) + jnp.where(p < 3, 8, 0))
        load_sinv.wait()
        ring(R_SINV, 0)
        ring(R_SINV2, 0)
        load_idx.wait()
        own_index = idx[...]
        gi[z, 0] = own_index
        for k in Z_ORDER:
            send(gi.at[z, 0], gi.at[z, 0], X_IDX, z_peer(k)[1])

        @pl.when(p == 0)
        def _():
            gi[z, 2] = own_index

        @pl.when(p == 3)
        def _():
            gi[z, 1] = own_index

        @pl.when(p < 3)
        def _():
            send(gi.at[z, 0], gi.at[z, 2], X_UP, (p + 1, front))

        @pl.when(p > 0)
        def _():
            send(gi.at[z, 0], gi.at[z, 1], X_DOWN, (p - 1, front))

    load_cc.wait()
    load_rhs.wait()
    flat = rhs[...].reshape(64, CELLS).astype(BF16)
    towards = jnp.zeros((64, 2 * FACE), F32)
    faces = [jnp.zeros((64, 2 * FACE), F32) for _ in range(2)]
    link = jnp.concatenate([cc[0], cc[1]], axis=1)
    starts = (0, CELLS - FACE)
    for block in range(5):
        rows = pl.ds(block * BLOCK, BLOCK)
        load_inv[block].wait()
        real = dot(inv[0, rows], link)
        imag = dot(inv[1, rows], link)
        part = jnp.concatenate(
            [real[:, :FACE] - imag[:, FACE:], real[:, FACE:] + imag[:, :FACE]], axis=1
        ).astype(BF16)
        w[rows] = part
        some = flat[:, block * BLOCK : (block + 1) * BLOCK]
        towards = towards + dot(some, part)
        for side, start in enumerate(starts):
            cols = pl.ds(start, FACE)
            both = jnp.concatenate([inv[0, rows, cols], inv[1, rows, cols]], axis=1)
            faces[side] = faces[side] + dot(some, both)
        if block == 0:
            tst[0] = part[:FACE]
        if block == 1:
            begin()

            @pl.when(p > 0)
            def _():
                send(tst.at[0], gm.at[S_T, z], X_T, (p - 1, front))
        if block == 3:
            ring(R_SINV, 1)
            ring(R_SINV2, 1)
        if block == 4:
            @pl.when(p > 0)
            def _():
                wait(gi.at[0, 0], rsem.at[X_UP])

            @pl.when(p < 3)
            def _():
                wait(gi.at[0, 0], rsem.at[X_DOWN])

            for k in Z_ORDER:
                send(gi.at[z, pl.ds(1, 2)], gi.at[z, pl.ds(1, 2)], X_IDX2, z_peer(k)[1])
    tst[1] = w[pl.ds(CELLS - FACE, FACE)]

    def combine(value):
        return jnp.concatenate(
            [value[:32, :FACE] - value[32:, FACE:], value[32:, :FACE] + value[:32, FACE:]], axis=0
        )

    load_bs.wait()
    place = pl.ds(pl.multiple_of(lax.rem(z, 4) * 32 + c * 16, 16), 16)
    for part in range(2):
        bst[part, place] = bs[part]
    given = jnp.concatenate([jnp.transpose(bst[0]), jnp.transpose(bst[1])], axis=0)
    face_first, face_last = combine(faces[0]), combine(faces[1])

    def put(item, value):
        for other in range(8):
            stage[other, item] = jnp.concatenate(
                [value[4 * other : 4 * other + 4], value[32 + 4 * other : 36 + 4 * other]], axis=0
            )

    put(0, combine(towards))
    put(1, given)
    for k in Z_ORDER:
        other, device = z_peer(k)
        send(stage.at[other, pl.ds(0, 2)], kb.at[z, pl.ds(0, 2)], X_BASE, device)

    @pl.when(p == 2)
    def _():
        send(tst.at[1], gm.at[S_T, z], X_T, (3, front))

    @pl.when(p < 2)
    def _():
        send(tst.at[1], gm.at[S_T2, z], X_T2, (p + 1, front))

    ring(R_SINV, 2)
    ring(R_SINV2, 2)
    wait(gm.at[S_T, 0], rsem.at[X_T])

    @pl.when(p > 0)
    def _():
        ring(S_T, 0)

    ahead_t = gm[S_T, z]
    put(2, jnp.where(p < 3, face_last, face_first))
    put(3, jnp.where(p == 0, combine(dot(face_last.astype(BF16), ahead_t)), face_first))
    for k in Z_ORDER:
        other, device = z_peer(k)
        send(stage.at[other, pl.ds(2, 2)], kb.at[z, pl.ds(2, 2)], X_BASE2, device)
    kb[z] = stage[z]
    outs = []
    for side, start in enumerate(starts):
        total = jnp.zeros((2 * FACE, 2 * FACE), F32)
        for block in range(5):
            rows, cols = pl.ds(block * BLOCK, BLOCK), pl.ds(start, FACE)
            both = jnp.concatenate([inv[0, rows, cols], inv[1, rows, cols]], axis=1)
            total = total + lax.dot_general(
                link[block * BLOCK : (block + 1) * BLOCK], both, TN, preferred_element_type=F32
            )
        outs.append(
            jnp.concatenate(
                [total[:FACE, :FACE] - total[FACE:, FACE:], total[:FACE, FACE:] + total[FACE:, :FACE]], axis=1
            )
        )
    gm[S_O, z] = jnp.where(p < 3, outs[1], outs[0]).astype(BF16)
    gm[S_O2, z] = outs[0].astype(BF16)
    low, high = pl.ds(0, FACE), pl.ds(CELLS - FACE, FACE)
    d_ff = jnp.concatenate([inv[0, low, low], inv[1, low, low]], axis=1)
    gm[S_DFF, z] = d_ff
    gm[S_D2, z] = jnp.concatenate([inv[0, high, low], inv[1, high, low]], axis=1)
    gm[S_D, z] = jnp.where(p < 3, jnp.concatenate([inv[0, low, high], inv[1, low, high]], axis=1), d_ff)
    ring(R_SINV, 3)
    ring(R_SINV2, 3)

    @pl.when(p == 0)
    def _():
        tall = jnp.concatenate([outs[1][:, :FACE], outs[1][:, FACE:]], axis=0).astype(BF16)
        both = dot(tall, ahead_t)
        gm[S_T, z] = jnp.concatenate(
            [both[:FACE, :FACE] - both[FACE:, FACE:], both[FACE:, :FACE] + both[:FACE, FACE:]], axis=1
        ).astype(BF16)
        ring(S_T, 0)

    @pl.when(p > 0)
    def _():
        ring(S_D, 0)

    ring(S_O, 0)

    unknown = lax.broadcasted_iota(jnp.int32, (SEP, FACE), 0)

    def select(dst, item, by_row=False):
        for leaf in range(8):
            row = gi[leaf, item]
            if by_row:
                row = ((row >> 8) * 2 + ((row >> 4) & 1)) * 128 + ((row >> 5) & 7) * 16 + (row & 15)
            dst[:, leaf * FACE : (leaf + 1) * FACE] = jnp.where(unknown == row, 1.0, 0.0).astype(BF16)

    wait(gi.at[pl.ds(0, 7), 0], rsem.at[X_IDX])
    select(ptb, 0)

    sign = jnp.where(lax.broadcasted_iota(jnp.int32, (8, SEP), 0) < 4, -1.0, 1.0)

    def leafwise(vector, slot):
        parts = [dot(vector[:, leaf * FACE : (leaf + 1) * FACE], got[leaf] if slot is None else gm[slot, leaf]) for leaf in range(8)]
        direct = jnp.concatenate([v[:, :FACE] for v in parts], axis=1)
        crossed = jnp.concatenate([v[:, FACE:] for v in parts], axis=1)
        return direct + sign * jnp.roll(crossed, 4, axis=0)

    def fold(value):
        half = value.shape[1] // 2
        return jnp.concatenate([value[:, :half], value[:, half:]], axis=0).astype(BF16)

    def unfold(value):
        value = value.astype(F32)
        return jnp.concatenate([value[:8], value[8:]], axis=1)

    def scatter(value, matrix):
        return lax.dot_general(value.astype(BF16), matrix[...], NT, preferred_element_type=F32)

    def gather(value):
        return dot(value.astype(BF16), pto[...])

    def solve(turn, arrived, before, meanwhile):
        before()
        wait(pbuf.at[turn, pl.ds(0, arrived)], rsem.at[X_PART + turn])
        total = pbuf[turn, 0].astype(F32)
        for other in range(1, 8):
            total = total + pbuf[turn, other].astype(F32)
        reduced = unfold(total).astype(BF16)
        both = lax.dot_general(reduced, gs[...].reshape(2 * FACE, SEP), NT, preferred_element_type=F32)
        mine = both[:, :FACE] + sign[:, :FACE] * jnp.roll(both[:, FACE:], 4, axis=0)
        sbuf[turn, g] = mine
        for k in G_ORDER[:7]:
            send(sbuf.at[turn, g], sbuf.at[turn, g], X_SOL + turn, g_peer(k, p))
        meanwhile()
        wait(sbuf.at[turn, pl.ds(0, 7)], rsem.at[X_SOL + turn])
        return jnp.concatenate([sbuf[turn, other] for other in range(8)], axis=1)

    def onward(face, matrix, slot, which, turn, panel):
        face_low = face.astype(BF16)
        pout[which] = fold(-scatter(leafwise(face_low, slot), matrix))
        for k in G_ORDER:
            send(pout.at[which], pbuf.at[turn, g], X_PART + turn, g_peer(k, panel))
        yout[which] = fold(face)
        send(yout.at[which], yin.at[turn], X_Y + turn, (panel, front))

    def faces_back():
        for item in range(2):
            face = unfold(yin[item + 1])
            for leaf in range(8):
                hstage[leaf, item] = face[:, leaf * FACE : (leaf + 1) * FACE]
        for k in Z_ORDER:
            other, device = z_peer(k)
            send(hstage.at[other], hk.at[z], X_FACES, device)
        hk[z] = hstage[z]

    def through(o_slot, t_slot):
        for leaf in range(8):
            out = gm[o_slot, leaf]
            both = dot(jnp.concatenate([out[:, :FACE], out[:, FACE:]], axis=0), gm[t_slot, leaf])
            got[leaf] = jnp.concatenate(
                [both[:FACE, :FACE] - both[FACE:, FACE:], both[FACE:, :FACE] + both[:FACE, FACE:]], axis=1
            ).astype(BF16)

    def onward_folded(pick, acc, matrix, o_slot, which, turn, panel):
        pout[which] = fold(scatter(leafwise(pick, None) - acct[...], matrix))
        for k in G_ORDER:
            send(pout.at[which], pbuf.at[turn, g], X_PART + turn, g_peer(k, panel))
        yout[which] = fold(acc[...] - leafwise(pick, o_slot))
        send(yout.at[which], yin.at[turn], X_Y + turn, (panel, front))

    first_set(1)
    wait(kb.at[pl.ds(0, 7), pl.ds(0, 2)], rsem.at[X_BASE])
    own = -scatter(jnp.concatenate([kb[leaf, 0] for leaf in range(8)], axis=1), ptb)
    given_low = (kb[0, 1] + kb[1, 1]) + (kb[2, 1] + kb[3, 1])
    given_high = (kb[4, 1] + kb[5, 1]) + (kb[6, 1] + kb[7, 1])
    own = own + jnp.concatenate(
        [jnp.where(x == other // 2, given_low if other % 2 == 0 else given_high, 0.0) for other in range(8)], axis=1
    )
    pbuf[0, g] = fold(own)
    for k in G_ORDER[:7]:
        send(pbuf.at[0, g], pbuf.at[0, g], X_PART, g_peer(k, p))

    @pl.when(p == 0)
    def _():
        yin[1] = jnp.zeros((16, SEP // 2), BF16)

    @pl.when(p == 3)
    def _():
        yin[2] = jnp.zeros((16, SEP // 2), BF16)

    def base_before():
        select(pto, 0, by_row=True)
        ring_end(R_SINV)
        ring_end(R_SINV2)
        first_set(2)

    def base_meanwhile():
        wait(gi.at[pl.ds(0, 7), pl.ds(1, 2)], rsem.at[X_IDX2])

        @pl.when(p < 3)
        def _():
            select(pta, 1)

        @pl.when(p == 3)
        def _():
            select(pta, 2)

        first_set(3)
        wait(kb.at[pl.ds(0, 7), pl.ds(2, 2)], rsem.at[X_BASE2])
        acca[...] = jnp.concatenate([kb[leaf, 2] for leaf in range(8)], axis=1)
        accb[...] = jnp.concatenate([kb[leaf, 3] for leaf in range(8)], axis=1)

    stot[...] = solve(0, 7, base_before, base_meanwhile)

    @pl.when(p == 2)
    def _():
        wait(gm.at[S_T2, 0], rsem.at[X_T2])
        second_set(0)
        second_set(1)

    @pl.when(p > 0)
    def _():
        def meanwhile():
            wait(yin.at[1], rsem.at[X_Y + 1])
            ring_end(S_D)
            acca[...] += leafwise(unfold(yin[1]).astype(BF16), S_D)

            @pl.when(p > 1)
            def _():
                acct[...] = leafwise(acca[...].astype(BF16), S_T)

        @pl.when(p > 1)
        def _():
            ring_end(S_O)
            ring_end(S_T)
            through(S_O, S_T)

        stot[...] += solve(1, 8, lambda: None, meanwhile)

    @pl.when(p == 0)
    def _():
        pick = gather(stot[...]).astype(BF16)
        ring_end(S_T)
        pout[0] = fold(scatter(leafwise(pick, S_T) - accb[...], pta))
        for k in G_ORDER:
            send(pout.at[0], pbuf.at[1, g], X_PART + 1, g_peer(k, 1))
        ring_end(S_O)
        yout[0] = fold(acca[...] - leafwise(pick, S_O))
        send(yout.at[0], yin.at[1], X_Y + 1, (1, front))
        sides = rhs[...].reshape(64, CELLS).astype(BF16)
        links = jnp.concatenate([cc[0], cc[1]], axis=1)
        for block in range(5):
            cols = pl.ds(block * BLOCK, BLOCK)
            real = dot(sides, inv[0, :, cols])
            imag = dot(sides, inv[1, :, cols])
            out_ref[0, :, cols] = real[:32] - imag[32:]
            out_ref[1, :, cols] = real[32:] + imag[:32]
            by_real = lax.dot_general(links, inv[0, :, cols], TN, preferred_element_type=F32)
            by_imag = lax.dot_general(links, inv[1, :, cols], TN, preferred_element_type=F32)
            whole[:FACE, cols] = (by_real[:FACE] - by_imag[FACE:]).astype(BF16)
            whole[FACE:, cols] = (by_imag[:FACE] + by_real[FACE:]).astype(BF16)

    @pl.when(p == 1)
    def _():
        ring_end(S_O)
        ring_end(S_T)
        onward(acca[...] - leafwise(gather(stot[...]).astype(BF16), S_O), pta, S_T, 0, 1, 2)

    @pl.when(p > 1)
    def _():
        onward_folded(gather(stot[...]).astype(BF16), acca, pta, S_O, 0, turn_ahead, ahead)

    @pl.when(p == 1)
    def _():
        wait(gm.at[S_T2, 0], rsem.at[X_T2])
        second_set(0)
        second_set(1)

    @pl.when(middle)
    def _():
        select(ptz, 2)
        second_set(2)
        second_set(3)
        for slot in SECOND_SET:
            ring_end(slot)
        accb[...] += leafwise(unfold(yin[1]).astype(BF16), S_DFF)
        through(S_O2, S_T2)

    @pl.when(p < 3)
    def _():
        def meanwhile():
            wait(yin.at[2], rsem.at[X_Y + 2])
            faces_back()

            @pl.when(p > 0)
            def _():
                accb[...] += leafwise(unfold(yin[2]).astype(BF16), S_D2)
                acct[...] = leafwise(accb[...].astype(BF16), S_T2)

        stot[...] += solve(2, 8, lambda: None, meanwhile)

    @pl.when(p == 3)
    def _():
        faces_back()

    picked = gather(stot[...])

    @pl.when(middle)
    def _():
        onward_folded(picked.astype(BF16), accb, ptz, S_O2, 1, 2, p - 1)

    own_sep = sbuf[0, g]
    own_sep = own_sep + jnp.where(p > 0, sbuf[1, g], 0.0)
    own_sep = own_sep + jnp.where(p < 3, sbuf[2, g], 0.0)
    for leaf in range(8):
        cols = slice(leaf * FACE, (leaf + 1) * FACE)
        fstage[leaf, 0] = picked[:, cols]
        fstage[leaf, 1] = own_sep
    for k in Z_ORDER:
        other, device = z_peer(k)
        send(fstage.at[other], fk.at[z], X_FINAL, device)
    fk[z] = fstage[z]

    def rows_of(ref, item):
        tops = [ref[other, item][:4] for other in range(8)]
        bottoms = [ref[other, item][4:] for other in range(8)]
        return jnp.concatenate(tops, axis=0), jnp.concatenate(bottoms, axis=0)

    def doubled(ref, item):
        re, im = rows_of(ref, item)
        return jnp.concatenate(
            [jnp.concatenate([re, -im], axis=1), jnp.concatenate([im, re], axis=1)], axis=0
        ).astype(BF16)

    wait(hk.at[pl.ds(0, 7)], rsem.at[X_FACES])

    @pl.when(p == 0)
    def _():
        face = doubled(hk, 1)
        for block in range(5):
            cols = pl.ds(block * BLOCK, BLOCK)
            both = dot(face, jnp.concatenate([inv[0, high, cols], inv[1, high, cols]], axis=0))
            out_ref[0, :, cols] += both[:32]
            out_ref[1, :, cols] += both[32:]

    wait(fk.at[pl.ds(0, 7)], rsem.at[X_FINAL])

    @pl.when(p == 0)
    def _():
        both = dot(doubled(fk, 0), whole[...])
        out_ref[0] -= both[:32]
        out_ref[1] -= both[32:]

    @pl.when(p > 0)
    def _():
        links = jnp.concatenate([cc[0], cc[1]], axis=1)
        side = rhs[...].reshape(64, CELLS) - lax.dot_general(
            doubled(fk, 0), links, NT, preferred_element_type=F32
        )
        add_low = jnp.concatenate(rows_of(hk, 0), axis=0)
        add_high = jnp.concatenate(rows_of(hk, 1), axis=0)
        side = jnp.concatenate(
            [side[:, :FACE] + add_low, side[:, FACE : CELLS - FACE], side[:, CELLS - FACE :] + add_high], axis=1
        ).astype(BF16)
        for block in range(5):
            cols = pl.ds(block * BLOCK, BLOCK)
            real = dot(side, inv[0, :, cols])
            imag = dot(side, inv[1, :, cols])
            out_ref[0, :, cols] = real[:32] - imag[32:]
            out_ref[1, :, cols] = real[32:] + imag[:32]

    for part, value in enumerate(rows_of(fk, 1)):
        bst[part] = jnp.transpose(value)
        sep_ref[part] = bst[part, pl.ds(pl.multiple_of(z * 16, 16), 16)]

    ring_left(R_SINV)
    ring_left(R_SINV2)
    ring_left(S_O)
    ring_left(S_T)
    wait(gi.at[pl.ds(0, 7), 0], ssem.at[X_IDX])
    wait(gi.at[pl.ds(0, 7), pl.ds(1, 2)], ssem.at[X_IDX2])
    wait(kb.at[pl.ds(0, 7), pl.ds(0, 2)], ssem.at[X_BASE])
    wait(kb.at[pl.ds(0, 7), pl.ds(0, 2)], ssem.at[X_BASE2])
    wait(hk.at[pl.ds(0, 7)], ssem.at[X_FACES])
    wait(fk.at[pl.ds(0, 7)], ssem.at[X_FINAL])
    wait(pbuf.at[0, pl.ds(0, 7)], ssem.at[X_PART])
    wait(sbuf.at[0, pl.ds(0, 7)], ssem.at[X_SOL])

    @pl.when(p > 0)
    def _():
        ring_left(S_D)
        wait(gi.at[0, 0], ssem.at[X_DOWN])
        wait(pbuf.at[2], ssem.at[X_PART + 2])
        wait(sbuf.at[1, pl.ds(0, 7)], ssem.at[X_SOL + 1])
        wait(yin.at[2], ssem.at[X_Y + 2])

    @pl.when(p < 3)
    def _():
        wait(gi.at[0, 0], ssem.at[X_UP])
        wait(pbuf.at[1], ssem.at[X_PART + 1])
        wait(sbuf.at[2, pl.ds(0, 7)], ssem.at[X_SOL + 2])
        wait(yin.at[1], ssem.at[X_Y + 1])

    @pl.when((p == 1) | (p == 3))
    def _():
        wait(tst.at[0], ssem.at[X_T])

    @pl.when(p == 2)
    def _():
        wait(tst, ssem.at[X_T])

    @pl.when(p < 2)
    def _():
        wait(tst.at[1], ssem.at[X_T2])

    @pl.when(middle)
    def _():
        for slot in SECOND_SET:
            ring_left(slot)


def local(leaf_rhs, sep_rhs, leaf_inverse, coupling, sep_index, sep_inverse):
    vmem = pl.BlockSpec(memory_space=pltpu.VMEM)
    hbm = pl.BlockSpec(memory_space=pl.ANY)
    leaf, sep = pl.pallas_call(
        kernel,
        out_shape=(jax.ShapeDtypeStruct((2, 32, CELLS), F32), jax.ShapeDtypeStruct((2, 16, 32), F32)),
        in_specs=[hbm] * 6,
        out_specs=(vmem, vmem),
        scratch_shapes=[
            pltpu.VMEM((2, 32, CELLS), F32),
            pltpu.VMEM((2, 16, 32), F32),
            pltpu.VMEM((2, CELLS, CELLS), BF16),
            pltpu.VMEM((2, CELLS, FACE), BF16),
            pltpu.VMEM((1, FACE), jnp.int32),
            pltpu.VMEM((CELLS, 2 * FACE), BF16),
            pltpu.VMEM((2, FACE, 2 * FACE), BF16),
            pltpu.VMEM((7, 8, FACE, 2 * FACE), BF16),
            pltpu.VMEM((2, 8, 16, SEP), BF16),
            pltpu.VMEM((8, 3, 1, FACE), jnp.int32),
            pltpu.VMEM((SEP, SEP), BF16),
            pltpu.VMEM((SEP, SEP), BF16),
            pltpu.VMEM((SEP, SEP), BF16),
            pltpu.VMEM((SEP, SEP), BF16),
            pltpu.VMEM((8, 4, 8, FACE), F32),
            pltpu.VMEM((8, 4, 8, FACE), F32),
            pltpu.VMEM((3, 8, 16, SEP // 2), BF16),
            pltpu.VMEM((2, 16, SEP // 2), BF16),
            pltpu.VMEM((3, 8, 8, FACE), F32),
            pltpu.VMEM((2, 16, SEP // 2), BF16),
            pltpu.VMEM((3, 16, SEP // 2), BF16),
            pltpu.VMEM((2, FACE, 32), F32),
            pltpu.VMEM((8, 2, 8, FACE), F32),
            pltpu.VMEM((8, 2, 8, FACE), F32),
            pltpu.VMEM((8, 2, 8, FACE), F32),
            pltpu.VMEM((8, 2, 8, FACE), F32),
            pltpu.VMEM((8, SEP), F32),
            pltpu.VMEM((8, SEP), F32),
            pltpu.VMEM((8, SEP), F32),
            pltpu.VMEM((8, SEP), F32),
            pltpu.VMEM((8, FACE, 2 * FACE), BF16),
            pltpu.VMEM((2 * FACE, CELLS), BF16),
            pltpu.SemaphoreType.DMA((10,)),
            pltpu.SemaphoreType.DMA((X_COUNT,)),
            pltpu.SemaphoreType.DMA((X_COUNT,)),
            pltpu.SemaphoreType.DMA((9, 2, 4)),
            pltpu.SemaphoreType.DMA((9, 2, 4)),
        ],
        compiler_params=pltpu.CompilerParams(
            collective_id=0, has_side_effects=True, vmem_limit_bytes=56 * 2**20
        ),
    )(
        leaf_rhs[0, 0], sep_rhs[0].transpose(0, 2, 1), leaf_inverse[0, 0], coupling[0, 0], sep_index[0],
        sep_inverse[0].transpose(0, 2, 1)
    )
    return leaf[None, None], sep.transpose(0, 2, 1)[None]


def solution(mesh):
    in_specs = (
        P("panel", "front", None, None, None),
        P("panel", None, None, "front"),
        P("panel", "front", None, None, None),
        P("panel", "front", None, None, None),
        P("panel", "front", None),
        P("panel", None, None, "front"),
    )
    out_specs = (P("panel", "front", None, None, None), P("panel", None, None, "front"))
    return jax.shard_map(local, mesh=mesh, in_specs=in_specs, out_specs=out_specs, check_vma=False)
```
